32 devices in a mesh: dp: 16 (over z, y, x), mp: 2 (over core).
Axes of the slice: x: 2, y: 2, z: 4, core: 2. Of those that a mesh axis runs over, the one named last changes fastest.
Arguments:
- queries: bfloat16 [2048, 8192], P('dp', 'mp'), may hold values from -6 to 6
- query_gain: float32 [8192], P('mp'), may hold values from 0.4 to 1.6
- keys: bfloat16 [2048, 8192], P('dp', 'mp'), may hold values from -24 to 24
- values: bfloat16 [2048, 8192], P('dp', 'mp'), may hold values from -6 to 6
- neighbours: int32 [32, 2], P('dp'), may hold values from 0 to 15, as said below
- d_out: bfloat16 [2048, 8192], P('dp', 'mp'), may hold values from -6 to 6
Outputs:
- attended: bfloat16 [2048, 8192], P('dp', 'mp')
- d_queries: bfloat16 [2048, 8192], P('dp', 'mp')
- d_keys: bfloat16 [2048, 8192], P('dp', 'mp')
- d_values: bfloat16 [2048, 8192], P('dp', 'mp')
The draws below stay inside these ranges and needn't reach their ends.
Inputs may be any that keep to these rules, and one draw needn't show every extreme that they name: The two neighbours of group c are two different blocks among (c // 2 + k) mod 16 for k = -2, -1, 0, 1, 2; the four neighbours named by the groups of one index of dp are four different blocks.
All inputs are finite; a program needn't handle non-finite values.
Results may differ from the reference program's by a relative error of at most 0.0071.
Values may be sent and summed in bfloat16 or wider, within the bound.
No kernel may reach another device: no remote copies, remote signals or barrier semaphores. Data moves between devices by JAX's collectives and lax.ppermute only.
A program may use at most 128 MiB of HBM per device.

```python
import jax
import jax.numpy as jnp
from jax import lax

HEADS = 64
HS = 128
GROUP = 64
NEIGH = 2
NLEN = 128
CH_DEV = 2
FEAT = 8192
GROUPS = 32
TOKENS = 2048
CACHED = 16
BLOCK_ROWS = 2048


def draw_queries(key, part):
    result = jnp.clip(jax.random.normal(jax.random.fold_in(key, 30), (TOKENS, FEAT), jnp.float32), -6.0, 6.0)
    return result.astype(jnp.bfloat16)


def draw_keys(key, part):
    result = jnp.clip(jax.random.normal(jax.random.fold_in(key, 40), (BLOCK_ROWS, FEAT), jnp.float32), -6.0, 6.0)
    return result.astype(jnp.bfloat16)


def draw_neighbours(key, part):
    random_first = jax.random.randint(jax.random.fold_in(key, 11), (GROUPS,), 0, 5)
    stride = jax.random.randint(jax.random.fold_in(key, 12), (GROUPS,), 1, 5)
    random_second = (random_first + stride) % 5
    owner = jnp.arange(GROUPS, dtype=jnp.int32) // CH_DEV
    within = jnp.arange(GROUPS, dtype=jnp.int32) % CH_DEV
    rotation = jax.random.randint(jax.random.fold_in(key, 13), (CACHED,), 0, 5)[owner]
    cover_first = (2 * within + rotation) % 5
    cover_second = (2 * within + 1 + rotation) % 5
    covering = within < 3
    first = jnp.where(covering, cover_first, random_first)
    second = jnp.where(covering, cover_second, random_second)
    offsets = jnp.stack([first, second], axis=1).astype(jnp.int32) - 2
    return ((owner[:, None] + offsets) % CACHED).astype(jnp.int32)


def block_scale(own_key, shape, shards, smallest, largest):
    loudness, own = 1.0, jax.random.fold_in(own_key, 6)
    for axis_at, blocks in shards:
        draws = jnp.exp(jax.random.uniform(jax.random.fold_in(own, axis_at), (blocks,), jnp.float32, smallest / len(shards), largest / len(shards)))
        loudness = loudness * jnp.repeat(draws, shape[axis_at] // blocks).reshape([-1 if axis == axis_at else 1 for axis in range(len(shape))])
    return loudness


def noise(own_key, extent, scale, limit, pieces=(), kind=jnp.bfloat16):
    entries = scale * jax.random.normal(own_key, extent, jnp.float32)
    if pieces:
        entries = entries * block_scale(own_key, extent, pieces, -0.22, 0.18)
    return jnp.clip(entries, -limit, limit).astype(kind)


def setup_inputs(seed: int = 0) -> dict:
    key_of = jax.random.split(jax.random.key(seed), 7)
    queries = draw_queries(jax.random.fold_in(key_of[6], 71), 0)
    query_gain = jnp.clip(1.0 + 0.12 * jax.random.normal(key_of[1], (FEAT,), jnp.float32), 0.4, 1.6)
    keys = draw_keys(jax.random.fold_in(key_of[6], 71), 0)
    values = noise(key_of[3], (BLOCK_ROWS, FEAT), 1.0, 6.0, ((0, 16), (1, 2)))
    neighbours = draw_neighbours(jax.random.fold_in(key_of[6], 71), 0)
    d_out = noise(key_of[5], (TOKENS, FEAT), 1.0, 6.0, ((0, 16), (1, 2)))
    return {"queries": queries, "query_gain": query_gain, "keys": keys, "values": values, "neighbours": neighbours, "d_out": d_out}


EPSILON = 1e-06

def reference(queries, query_gain, keys, values, neighbours, d_out):
    width = HEADS * HS
    rows = CH_DEV * GROUP
    scaling = 1.0 / HS ** 0.5
    inputs_all = queries.astype(jnp.float32)
    inverse_all = lax.rsqrt(lax.optimization_barrier(jnp.mean(inputs_all * inputs_all, axis=1, keepdims=True)) + EPSILON)
    normed_all = (inputs_all * query_gain * inverse_all).astype(jnp.bfloat16)
    key_blocks = keys.reshape(CACHED, NLEN, width)
    value_blocks = values.reshape(CACHED, NLEN, width)

    def device_step(carry, index):
        key_acc, value_acc = carry
        normed = lax.dynamic_slice_in_dim(normed_all, index * rows, rows, 0)
        grads = lax.dynamic_slice_in_dim(d_out, index * rows, rows, 0)
        block_ids = lax.dynamic_slice_in_dim(neighbours, index * CH_DEV, CH_DEV, 0)
        near_keys = key_blocks[block_ids].reshape(CH_DEV, NEIGH * NLEN, HEADS, HS).astype(jnp.float32)
        near_values = value_blocks[block_ids].reshape(CH_DEV, NEIGH * NLEN, HEADS, HS).astype(jnp.float32)
        query_four = normed.reshape(CH_DEV, GROUP, HEADS, HS).astype(jnp.float32)
        grad_four = grads.reshape(CH_DEV, GROUP, HEADS, HS).astype(jnp.float32)
        scores = jnp.einsum('cqhd,ckhd->chqk', query_four, near_keys) * scaling
        probs = jax.nn.softmax(scores, axis=-1)
        probs_low = probs.astype(jnp.bfloat16).astype(jnp.float32)
        context = jnp.einsum('chqk,ckhd->cqhd', probs_low, near_values)
        attended = context.astype(jnp.bfloat16).reshape(rows, width)
        grad_probs = jnp.einsum('cqhd,ckhd->chqk', grad_four, near_values)
        centre = lax.optimization_barrier(jnp.sum(probs * grad_probs, axis=-1, keepdims=True))
        grad_scores = (probs * (grad_probs - centre)).astype(jnp.bfloat16).astype(jnp.float32)
        grad_normed = jnp.einsum('chqk,ckhd->cqhd', grad_scores, near_keys) * scaling
        key_terms = (jnp.einsum('chqk,cqhd->ckhd', grad_scores, query_four) * scaling).reshape(CH_DEV, NEIGH, NLEN, width)
        value_terms = jnp.einsum('chqk,cqhd->ckhd', probs_low, grad_four).reshape(CH_DEV, NEIGH, NLEN, width)
        local_ids = (block_ids - index + 2) % CACHED
        selector = (local_ids[:, :, None] == jnp.arange(5, dtype=jnp.int32)[None, None, :]).astype(jnp.float32)
        key_parts = jnp.einsum('cno,cnlf->olf', selector, key_terms, precision=lax.Precision.HIGHEST).astype(jnp.bfloat16)
        value_parts = jnp.einsum('cno,cnlf->olf', selector, value_terms, precision=lax.Precision.HIGHEST).astype(jnp.bfloat16)
        key_parts = lax.optimization_barrier(key_parts).astype(jnp.float32)
        value_parts = lax.optimization_barrier(value_parts).astype(jnp.float32)
        for offset in range(5):
            target = (index - 2 + offset) % CACHED
            key_acc = key_acc.at[target].add(key_parts[offset])
            value_acc = value_acc.at[target].add(value_parts[offset])
        return ((key_acc, value_acc), (attended, grad_normed.reshape(rows, width)))
    start = (jnp.zeros((CACHED, NLEN, width), jnp.float32), jnp.zeros((CACHED, NLEN, width), jnp.float32))
    (key_acc, value_acc), (attended, grad_normed) = lax.scan(device_step, start, jnp.arange(CACHED, dtype=jnp.int32))
    attended = attended.reshape(TOKENS, width)
    scaled_grad = grad_normed.reshape(TOKENS, width) * query_gain
    inner = lax.optimization_barrier(jnp.sum(scaled_grad * inputs_all, axis=1, keepdims=True))
    cubed = inverse_all * inverse_all * inverse_all
    d_queries = (inverse_all * scaled_grad - inputs_all * cubed * inner / width).astype(jnp.bfloat16)
    d_keys = key_acc.reshape(BLOCK_ROWS, width).astype(jnp.bfloat16)
    d_values = value_acc.reshape(BLOCK_ROWS, width).astype(jnp.bfloat16)
    return (attended, d_queries, d_keys, d_values)
```

```python
import functools

import jax
import jax.numpy as jnp
from jax import lax
from jax.experimental import pallas as pl
from jax.experimental.pallas import tpu as pltpu
from jax.sharding import PartitionSpec as P

HEADS = 64
HS = 128
GROUP = 64
NEIGH = 2
EPSILON = 1e-06
SCALING = 1.0 / HS**0.5
OFFSETS = (-2, -1, 0, 1, 2)
SLOTS = len(OFFSETS)
OWN = 2
LANES = 128
CHUNK = 4


def passed_along(block, distance):
    count = lax.axis_size("dp")
    route = [((i - distance) % count, i) for i in range(count)]
    return lax.ppermute(block, "dp", route)


def to_owners(parts):
    return [passed_along(parts[o], d) if d else parts[o] for o, d in enumerate(OFFSETS)]


def to_origins(parts):
    return [passed_along(parts[o], -d) if d else parts[o] for o, d in enumerate(OFFSETS)]


def dot_nt(a, b):
    return lax.dot_general(a, b, (((1,), (1,)), ((), ())), preferred_element_type=jnp.float32)


def dot_nn(a, b):
    return lax.dot_general(a, b, (((1,), (0,)), ((), ())), preferred_element_type=jnp.float32)


def dot_tn(a, b):
    return lax.dot_general(a, b, (((0,), (0,)), ((), ())), preferred_element_type=jnp.float32)


def head(refs, h):
    cols = slice(h * HS, (h + 1) * HS)
    return jnp.concatenate([r[:, cols] for r in refs], axis=0)


def lane_iota(rows):
    return lax.broadcasted_iota(jnp.int32, (rows, LANES), 1)


def forward_kernel(heads, *refs):
    q_refs, g_refs = refs[:SLOTS], refs[SLOTS : 2 * SLOTS]
    k_ref, v_ref = refs[2 * SLOTS : 2 * SLOTS + 2]
    ctx_refs = refs[2 * SLOTS + 2 : 3 * SLOTS + 2]
    stat_refs = refs[3 * SLOTS + 2 :]
    step = pl.program_id(0)
    rows = SLOTS * GROUP
    lane = lane_iota(rows)
    stats = jnp.zeros((rows, LANES), jnp.float32)
    for h in range(CHUNK):
        cols = slice(h * HS, (h + 1) * HS)
        q, g = head(q_refs, h), head(g_refs, h)
        k, v = k_ref[:, cols], v_ref[:, cols]
        scores = dot_nt(q, k) * SCALING
        top = jnp.max(scores, axis=1, keepdims=True)
        weights = jnp.exp(scores - top)
        total = jnp.sum(weights, axis=1, keepdims=True)
        grad_probs = dot_nt(g, v)
        centre = jnp.sum(weights * grad_probs, axis=1, keepdims=True)
        context = dot_nn(weights.astype(jnp.bfloat16), v).astype(jnp.bfloat16)
        for o in range(SLOTS):
            ctx_refs[o][:, cols] = context[o * GROUP : (o + 1) * GROUP]
        stats = jnp.where(lane == h, top, stats)
        stats = jnp.where(lane == heads + h, total, stats)
        stats = jnp.where(lane == 2 * heads + h, centre, stats)
    stats = pltpu.roll(stats, step * CHUNK, 1)

    @pl.when(step == 0)
    def _():
        for o in range(SLOTS):
            stat_refs[o][...] = stats[o * GROUP : (o + 1) * GROUP]

    @pl.when(step > 0)
    def _():
        for o in range(SLOTS):
            stat_refs[o][...] += stats[o * GROUP : (o + 1) * GROUP]


def combine_kernel(heads, groups, info_ref, *refs):
    stat_refs, back_refs, share_refs = refs[:SLOTS], refs[SLOTS : 2 * SLOTS], refs[2 * SLOTS :]
    shape = (GROUP, heads)
    tops = [r[:, 0:heads] for r in stat_refs]
    totals = [r[:, heads : 2 * heads] for r in stat_refs]
    centres = [r[:, 2 * heads : 3 * heads] for r in stat_refs]
    group_of = [jnp.full(shape, info_ref[o], jnp.int32) for o in range(SLOTS)]
    lowest = jnp.full(shape, -jnp.inf, jnp.float32)
    top_all, inv_all, centre_all = [], [], []
    for g in range(groups):
        top = lowest
        for o in range(SLOTS):
            top = jnp.maximum(top, jnp.where(group_of[o] == g, tops[o], lowest))
        total = jnp.zeros(shape, jnp.float32)
        centre = jnp.zeros(shape, jnp.float32)
        for o in range(SLOTS):
            mine = group_of[o] == g
            factor = jnp.where(mine, jnp.exp(jnp.where(mine, tops[o] - top, 0.0)), 0.0)
            total = total + totals[o] * factor
            centre = centre + centres[o] * factor
        top_all.append(top)
        inv_all.append(1.0 / total)
        centre_all.append(centre / total)
    fill = jnp.zeros((GROUP, LANES - 3 * heads), jnp.float32)
    rest = jnp.zeros((GROUP, LANES - heads), jnp.float32)
    for o in range(SLOTS):
        top, inv = tops[o], jnp.zeros(shape, jnp.float32)
        centre = jnp.zeros(shape, jnp.float32)
        for g in range(groups):
            mine = group_of[o] == g
            top = jnp.where(mine, top_all[g], top)
            inv = jnp.where(mine, inv_all[g], inv)
            centre = jnp.where(mine, centre_all[g], centre)
        share = jnp.exp(tops[o] - top) * inv
        back_refs[o][...] = jnp.concatenate([top, inv, centre, fill], axis=1)
        share_refs[o][...] = jnp.concatenate([share, rest], axis=1)


def backward_kernel(heads, *refs):
    q_refs, g_refs = refs[:SLOTS], refs[SLOTS : 2 * SLOTS]
    back_refs = refs[2 * SLOTS : 3 * SLOTS]
    k_ref, v_ref = refs[3 * SLOTS : 3 * SLOTS + 2]
    grad_refs = refs[3 * SLOTS + 2 : 4 * SLOTS + 2]
    dk_ref, dv_ref = refs[4 * SLOTS + 2 :]
    step = pl.program_id(0)
    back = jnp.concatenate([r[...] for r in back_refs], axis=0)
    back = pltpu.roll(back, (LANES - step * CHUNK) % LANES, 1)
    for h in range(CHUNK):
        cols = slice(h * HS, (h + 1) * HS)
        q, g = head(q_refs, h), head(g_refs, h)
        k, v = k_ref[:, cols], v_ref[:, cols]
        top = back[:, h : h + 1]
        inv = back[:, heads + h : heads + h + 1]
        centre = back[:, 2 * heads + h : 2 * heads + h + 1]
        probs = jnp.exp(dot_nt(q, k) * SCALING - top) * inv
        grad_scores = (probs * (dot_nt(g, v) - centre)).astype(jnp.bfloat16)
        grad = (dot_nn(grad_scores, k) * SCALING).astype(jnp.bfloat16)
        for o in range(SLOTS):
            grad_refs[o][:, cols] = grad[o * GROUP : (o + 1) * GROUP]
        dk_ref[:, cols] = (dot_tn(grad_scores, q) * SCALING).astype(jnp.bfloat16)
        dv_ref[:, cols] = dot_tn(probs.astype(jnp.bfloat16), g).astype(jnp.bfloat16)


def attended_kernel(groups, info_ref, *refs):
    ctx_refs, share_refs, out_ref = refs[:SLOTS], refs[SLOTS : 2 * SLOTS], refs[2 * SLOTS]
    step = pl.program_id(0)
    shift = (LANES - step * CHUNK) % LANES
    shares = [pltpu.roll(r[...], shift, 1) for r in share_refs]
    for g in range(groups):
        mine = [jnp.where(info_ref[o] == g, 1.0, 0.0) for o in range(SLOTS)]
        for h in range(CHUNK):
            cols = slice(h * HS, (h + 1) * HS)
            total = jnp.zeros((GROUP, HS), jnp.float32)
            for o in range(SLOTS):
                share = shares[o][:, h : h + 1] * mine[o]
                total = total + share * ctx_refs[o][:, cols].astype(jnp.float32)
            out_ref[g * GROUP : (g + 1) * GROUP, cols] = total.astype(jnp.bfloat16)


def gather_grad_kernel(groups, info_ref, *refs):
    grad_refs = refs[:SLOTS]
    q_ref, gain_ref, scaled_ref, inner_ref = refs[SLOTS:]
    step = pl.program_id(0)
    inners = []
    for g in range(groups):
        rows = slice(g * GROUP, (g + 1) * GROUP)
        mine = [jnp.where(info_ref[o] == g, 1.0, 0.0) for o in range(SLOTS)]
        total = mine[0] * grad_refs[0][...].astype(jnp.float32)
        for o in range(1, SLOTS):
            total = total + mine[o] * grad_refs[o][...].astype(jnp.float32)
        total = total * gain_ref[...]
        scaled_ref[rows] = total
        product = total * q_ref[rows].astype(jnp.float32)
        inners.append(jnp.sum(product, axis=1, keepdims=True))
    inner = jnp.broadcast_to(jnp.concatenate(inners, axis=0), inner_ref.shape)

    @pl.when(step == 0)
    def _():
        inner_ref[...] = inner

    @pl.when(step > 0)
    def _():
        inner_ref[...] += inner


def kernel_call(body, name, steps, in_specs, out_specs, out_shape, flops=0, moved=0):
    return pl.pallas_call(
        body,
        grid=(steps,),
        in_specs=in_specs,
        out_specs=out_specs,
        out_shape=out_shape,
        name=name,
        cost_estimate=pl.CostEstimate(flops=flops, bytes_accessed=moved, transcendentals=0),
        compiler_params=pltpu.CompilerParams(
            dimension_semantics=("arbitrary",), vmem_limit_bytes=32 * 1024 * 1024
        ),
    )


def local(queries, query_gain, keys, values, neighbours, d_out):
    rows, width = queries.shape
    heads = width // HS
    groups = rows // GROUP
    steps = heads // CHUNK
    count = lax.axis_size("dp")
    local_ids = (neighbours - lax.axis_index("dp") + 2) % count
    slot = jnp.arange(SLOTS, dtype=jnp.int32)
    uses = jnp.any(local_ids[:, :, None] == slot, axis=1)
    numbers = jnp.arange(groups, dtype=jnp.int32)[:, None]
    chosen = jnp.sum(jnp.where(uses, numbers, 0), axis=0)
    info = jnp.where(jnp.any(uses, axis=0), chosen, -1)

    def picked(array):
        return [lax.dynamic_slice_in_dim(array, chosen[o] * GROUP, GROUP, 0) for o in range(SLOTS)]

    g_slots = to_owners(picked(d_out))
    inputs = queries.astype(jnp.float32)
    squares = lax.psum(jnp.sum(inputs * inputs, axis=1), "mp")
    inverse = lax.rsqrt(squares / (HEADS * HS) + EPSILON)[:, None]
    normed = (inputs * query_gain * inverse).astype(jnp.bfloat16)
    q_slots = to_owners(picked(normed))

    wide = CHUNK * HS
    slot_block = pl.BlockSpec((GROUP, wide), lambda i: (0, i))
    cached_block = pl.BlockSpec((keys.shape[0], wide), lambda i: (0, i))
    rows_block = pl.BlockSpec((rows, wide), lambda i: (0, i))
    stat_block = pl.BlockSpec((GROUP, LANES), lambda i: (0, 0))
    info_block = pl.BlockSpec(memory_space=pltpu.SMEM)
    slot_shape = jax.ShapeDtypeStruct((GROUP, width), jnp.bfloat16)
    stat_shape = jax.ShapeDtypeStruct((GROUP, LANES), jnp.float32)
    cached_shape = jax.ShapeDtypeStruct(keys.shape, jnp.bfloat16)
    product = 2 * SLOTS * GROUP * keys.shape[0] * width
    array = GROUP * width * 2

    out = kernel_call(
        functools.partial(forward_kernel, heads),
        "forward",
        steps,
        [slot_block] * (2 * SLOTS) + [cached_block] * 2,
        [slot_block] * SLOTS + [stat_block] * SLOTS,
        [slot_shape] * SLOTS + [stat_shape] * SLOTS,
        3 * product,
        20 * array,
    )(*q_slots, *g_slots, keys, values)
    ctx_slots, stats = out[:SLOTS], out[SLOTS:]
    stats = to_origins(stats)
    ctx_slots = to_origins(ctx_slots)

    out = kernel_call(
        functools.partial(combine_kernel, heads, groups),
        "combine",
        1,
        [info_block] + [stat_block] * SLOTS,
        [stat_block] * (2 * SLOTS),
        [stat_shape] * (2 * SLOTS),
    )(info, *stats)
    back, shares = out[:SLOTS], out[SLOTS:]
    back = to_owners(back)

    out = kernel_call(
        functools.partial(backward_kernel, heads),
        "backward",
        steps,
        [slot_block] * (2 * SLOTS) + [stat_block] * SLOTS + [cached_block] * 2,
        [slot_block] * SLOTS + [cached_block] * 2,
        [slot_shape] * SLOTS + [cached_shape] * 2,
        5 * product,
        23 * array,
    )(*q_slots, *g_slots, *back, keys, values)
    grad_slots, (d_keys, d_values) = out[:SLOTS], out[SLOTS:]
    grad_slots = to_origins(grad_slots)

    attended = kernel_call(
        functools.partial(attended_kernel, groups),
        "attended",
        steps,
        [info_block] + [slot_block] * SLOTS + [stat_block] * SLOTS,
        rows_block,
        jax.ShapeDtypeStruct((rows, width), jnp.bfloat16),
        0,
        7 * array,
    )(info, *ctx_slots, *shares)

    scaled_grad, inner = kernel_call(
        functools.partial(gather_grad_kernel, groups),
        "gather_grad",
        steps,
        [info_block]
        + [slot_block] * SLOTS
        + [rows_block, pl.BlockSpec((1, wide), lambda i: (0, i))],
        [rows_block, pl.BlockSpec((rows, LANES), lambda i: (0, 0))],
        [
            jax.ShapeDtypeStruct((rows, width), jnp.float32),
            jax.ShapeDtypeStruct((rows, LANES), jnp.float32),
        ],
        0,
        11 * array,
    )(info, *grad_slots, queries, query_gain[None, :])
    inner = lax.psum(inner[:, 0], "mp")
    cubed = inverse * inverse * inverse
    d_queries = (inverse * scaled_grad - inputs * cubed * inner[:, None] / (HEADS * HS)).astype(
        jnp.bfloat16
    )
    return (attended, d_queries, d_keys, d_values)


def solution(mesh):
    placed = (P("dp", "mp"), P("mp"), P("dp", "mp"), P("dp", "mp"), P("dp", None), P("dp", "mp"))
    return jax.shard_map(
        local,
        mesh=mesh,
        in_specs=placed,
        out_specs=(P("dp", "mp"), P("dp", "mp"), P("dp", "mp"), P("dp", "mp")),
        check_vma=False,
    )
```

```python
import functools

import jax
import jax.numpy as jnp
from jax import lax
from jax.experimental import pallas as pl
from jax.experimental.pallas import tpu as pltpu
from jax.sharding import PartitionSpec as P

HEADS = 64
HS = 128
GROUP = 64
FEAT = HEADS * HS
EPSILON = 1e-06
SCALING = 1.0 / HS**0.5
LANES = 128
CHUNK = 8
WIDE = CHUNK * HS
SLOTS = 5
OWN = (0, 2)
PARTNER = (1, 3, 4)


def routes(count):
    def side(i):
        return -4 if i & 2 == 0 else 4

    diagonal = (-3, -1, 1, 3)
    return {
        "y": [(i, i ^ 2) for i in range(count)],
        2: [(i, i ^ 1) for i in range(count)],
        3: [(i, (i + side(i)) % count) for i in range(count)],
        4: [(i, (i + diagonal[i & 3]) % count) for i in range(count)],
    }


def sent(array, route):
    return lax.ppermute(array, "dp", route)


def out_and_back(count):
    route = routes(count)
    back = {s: [(b, a) for a, b in route[s]] for s in (2, 3, 4)}

    def go(parts):
        return [sent(p, route[s]) if s >= 2 else p for s, p in enumerate(parts)]

    def come(parts):
        return [sent(p, back[s]) if s >= 2 else p for s, p in enumerate(parts)]

    return go, come, functools.partial(sent, route=route["y"])


def dot(a, b, left, right):
    return lax.dot_general(a, b, (((left,), (right,)), ((), ())), preferred_element_type=jnp.float32)


def group_numbers(place_ref, near_ref, count, groups):
    place = place_ref[0]
    one = 1 - 2 * (place & 1)
    two = 2 - 2 * (place & 2)
    numbers = []
    for offset in (0, two, one, -two, -one):
        block = lax.rem(place + offset + count, count)
        number = jnp.int32(-1)
        for g in range(groups):
            used = (near_ref[g, 0] == block) | (near_ref[g, 1] == block)
            number = jnp.where(used, g, number)
        numbers.append(number)
    return numbers


def rows_of(number):
    return pl.ds(pl.multiple_of(jnp.maximum(number, 0) * GROUP, GROUP), GROUP)


def lane_partial(x):
    total = x[:, 0:LANES]
    for t in range(1, x.shape[1] // LANES):
        total = total + x[:, t * LANES : (t + 1) * LANES]
    return total


def to_row(x):
    return jnp.sum(x.T, axis=0, keepdims=True)


def to_columns(row):
    return jnp.broadcast_to(row, (row.shape[1], row.shape[1])).T


def prepare_grads_kernel(count, groups, place_ref, near_ref, g_ref, q_ref, *refs):
    slot_refs, squares_ref, total_ref = refs[:SLOTS], refs[SLOTS], refs[SLOTS + 1]
    numbers = group_numbers(place_ref, near_ref, count, groups)
    for s in range(SLOTS):
        slot_refs[s][...] = g_ref[rows_of(numbers[s])]
    step = pl.program_id(0)
    x = q_ref[...].astype(jnp.float32)
    partial = lane_partial(x * x)

    @pl.when(step == 0)
    def _():
        total_ref[...] = partial

    @pl.when(step > 0)
    def _():
        total_ref[...] += partial

    @pl.when(step == pl.num_programs(0) - 1)
    def _():
        squares_ref[...] = to_row(total_ref[...])


def inverse_columns(squares_ref):
    return to_columns(lax.rsqrt(squares_ref[...] / FEAT + EPSILON))


def prepare_queries_kernel(count, groups, place_ref, near_ref, q_ref, gain_ref, squares_ref, *refs):
    slot_refs, normed_ref = refs[:SLOTS], refs[SLOTS]
    numbers = group_numbers(place_ref, near_ref, count, groups)
    inverse = inverse_columns(squares_ref)
    for t in range(q_ref.shape[1] // LANES):
        cols = slice(t * LANES, (t + 1) * LANES)
        x = q_ref[:, cols].astype(jnp.float32)
        normed_ref[:, cols] = (x * gain_ref[:, cols] * inverse).astype(jnp.bfloat16)
    for s in range(SLOTS):
        slot_refs[s][...] = normed_ref[rows_of(numbers[s])]


def head(refs, slots, h):
    cols = slice(h * HS, (h + 1) * HS)
    return jnp.concatenate([refs[s][:, cols] for s in slots], axis=0)


def paired(stats, left, right):
    return jnp.concatenate([stats[left], stats[right]], axis=1)


def scores_kernel(*refs):
    q_refs, k_refs, stat_refs = refs[:SLOTS], refs[SLOTS : SLOTS + 2], refs[SLOTS + 2 :]
    for slots, k_ref in zip((OWN, PARTNER), k_refs):
        tops, totals = [], []
        for h in range(CHUNK):
            cols = slice(h * HS, (h + 1) * HS)
            scores = dot(k_ref[:, cols], head(q_refs, slots, h), 1, 1) * SCALING
            top = jnp.max(scores, axis=0, keepdims=True)
            tops.append(top)
            totals.append(jnp.sum(jnp.exp(scores - top), axis=0, keepdims=True))
        tops = jnp.concatenate(tops, axis=0)
        totals = jnp.concatenate(totals, axis=0)
        for at, s in enumerate(slots):
            lanes = slice(at * GROUP, (at + 1) * GROUP)
            stat_refs[s][...] = jnp.concatenate([tops[:, lanes], totals[:, lanes]], axis=1)


def combine_scores_kernel(count, groups, place_ref, near_ref, *refs):
    stat_refs, back_refs = refs[:SLOTS], refs[SLOTS:]
    numbers = group_numbers(place_ref, near_ref, count, groups)
    heads = stat_refs[0].shape[0]
    shape = (heads, GROUP)
    tops = [r[:, 0:GROUP] for r in stat_refs]
    totals = [r[:, GROUP : 2 * GROUP] for r in stat_refs]
    number_of = [jnp.full(shape, n, jnp.int32) for n in numbers]
    lowest = jnp.full(shape, -jnp.inf, jnp.float32)
    zero = jnp.zeros(shape, jnp.float32)
    merged = []
    for g in range(groups):
        top, total = lowest, zero
        for s in range(SLOTS):
            top = jnp.maximum(top, jnp.where(number_of[s] == g, tops[s], lowest))
        for s in range(SLOTS):
            mine = number_of[s] == g
            factor = jnp.exp(jnp.where(mine, tops[s] - top, zero))
            total = total + jnp.where(mine, totals[s] * factor, zero)
        merged.append((top, 1.0 / total))
    for s in range(SLOTS):
        top, inv = tops[s], zero
        for g in range(groups):
            mine = number_of[s] == g
            top = jnp.where(mine, merged[g][0], top)
            inv = jnp.where(mine, merged[g][1], inv)
        back_refs[s][...] = jnp.concatenate([top, inv], axis=1)


def combine_centres_kernel(count, groups, place_ref, near_ref, *refs):
    stat_refs, back_refs = refs[:SLOTS], refs[SLOTS:]
    numbers = group_numbers(place_ref, near_ref, count, groups)
    shape = stat_refs[0].shape
    number_of = [jnp.full(shape, n, jnp.int32) for n in numbers]
    zero = jnp.zeros(shape, jnp.float32)
    for g in range(groups):
        total = zero
        for s in range(SLOTS):
            total = total + jnp.where(number_of[s] == g, stat_refs[s][...], zero)
        for s in range(SLOTS):
            here = zero if g == 0 else back_refs[s][...]
            back_refs[s][...] = jnp.where(number_of[s] == g, total, here)


def stat_rows(stat_refs, slots, half):
    lanes = slice(half * GROUP, (half + 1) * GROUP)
    return jnp.concatenate([stat_refs[s][:, lanes] for s in slots], axis=1)


def probs_of(k, q, top, inv):
    return jnp.exp(dot(k, q, 1, 1) * SCALING - top) * inv


def context_kernel(*refs):
    q_refs, g_refs, back_refs = (refs[i * SLOTS : (i + 1) * SLOTS] for i in range(3))
    k_refs, v_refs = refs[3 * SLOTS : 3 * SLOTS + 2], refs[3 * SLOTS + 2 : 3 * SLOTS + 4]
    rest = refs[3 * SLOTS + 4 :]
    ctx_refs, centre_refs, dv_refs = rest[:SLOTS], rest[SLOTS : 2 * SLOTS], rest[2 * SLOTS :]
    for slots, k_ref, v_ref, dv_ref in zip((OWN, PARTNER), k_refs, v_refs, dv_refs):
        top, inv = stat_rows(back_refs, slots, 0), stat_rows(back_refs, slots, 1)
        centres = []
        for h in range(CHUNK):
            cols = slice(h * HS, (h + 1) * HS)
            q, g, v = head(q_refs, slots, h), head(g_refs, slots, h), v_ref[:, cols]
            probs = probs_of(k_ref[:, cols], q, top[h : h + 1], inv[h : h + 1])
            low = probs.astype(jnp.bfloat16)
            context = dot(low, v, 0, 0).astype(jnp.bfloat16)
            for at, s in enumerate(slots):
                ctx_refs[s][:, cols] = context[at * GROUP : (at + 1) * GROUP]
            centres.append(jnp.sum(probs * dot(v, g, 1, 1), axis=0, keepdims=True))
            dv_ref[:, cols] = dot(low, g, 1, 0).astype(dv_ref.dtype)
        centres = jnp.concatenate(centres, axis=0)
        empty = jnp.zeros((CHUNK, GROUP), jnp.float32)
        for at, s in enumerate(slots):
            lanes = slice(at * GROUP, (at + 1) * GROUP)
            centre_refs[s][...] = jnp.concatenate([centres[:, lanes], empty], axis=1)


def gradient_kernel(*refs):
    q_refs, g_refs, back_refs, centre_refs = (refs[i * SLOTS : (i + 1) * SLOTS] for i in range(4))
    k_refs, v_refs = refs[4 * SLOTS : 4 * SLOTS + 2], refs[4 * SLOTS + 2 : 4 * SLOTS + 4]
    rest = refs[4 * SLOTS + 4 :]
    grad_refs, dk_refs = rest[:SLOTS], rest[SLOTS:]
    for slots, k_ref, v_ref, dk_ref in zip((OWN, PARTNER), k_refs, v_refs, dk_refs):
        top, inv = stat_rows(back_refs, slots, 0), stat_rows(back_refs, slots, 1)
        centre = stat_rows(centre_refs, slots, 0)
        for h in range(CHUNK):
            cols = slice(h * HS, (h + 1) * HS)
            q, g = head(q_refs, slots, h), head(g_refs, slots, h)
            k, v = k_ref[:, cols], v_ref[:, cols]
            probs = probs_of(k, q, top[h : h + 1], inv[h : h + 1])
            low = (probs * (dot(v, g, 1, 1) - centre[h : h + 1])).astype(jnp.bfloat16)
            grad = (dot(low, k, 0, 0) * SCALING).astype(jnp.bfloat16)
            for at, s in enumerate(slots):
                grad_refs[s][:, cols] = grad[at * GROUP : (at + 1) * GROUP]
            dk_ref[:, cols] = (dot(low, q, 1, 0) * SCALING).astype(dk_ref.dtype)


def gathered(numbers, refs, g):
    total = None
    for s in range(SLOTS):
        part = jnp.where(numbers[s] == g, 1.0, 0.0) * refs[s][...].astype(jnp.float32)
        total = part if total is None else total + part
    return total


def attended_kernel(count, groups, place_ref, near_ref, *refs):
    ctx_refs, own_ref, far_ref, out_ref, dv_ref = (
        refs[:SLOTS], refs[SLOTS], refs[SLOTS + 1], refs[SLOTS + 2], refs[SLOTS + 3]
    )
    numbers = group_numbers(place_ref, near_ref, count, groups)
    for g in range(groups):
        out_ref[g * GROUP : (g + 1) * GROUP] = gathered(numbers, ctx_refs, g).astype(jnp.bfloat16)
    dv_ref[...] = (own_ref[...] + far_ref[...].astype(jnp.float32)).astype(jnp.bfloat16)


def inner_kernel(count, groups, place_ref, near_ref, *refs):
    grad_refs = refs[:SLOTS]
    q_ref, gain_ref, scaled_ref, inner_ref, total_ref = refs[SLOTS:]
    numbers = group_numbers(place_ref, near_ref, count, groups)
    step = pl.program_id(0)

    @pl.when(step == 0)
    def _():
        total_ref[...] = jnp.zeros_like(total_ref)

    for g in range(groups):
        rows = slice(g * GROUP, (g + 1) * GROUP)
        scaled = gathered(numbers, grad_refs, g) * gain_ref[...]
        scaled_ref[rows] = scaled
        total_ref[rows] += lane_partial(scaled * q_ref[rows].astype(jnp.float32))

    @pl.when(step == pl.num_programs(0) - 1)
    def _():
        inner_ref[...] = to_row(total_ref[...])


def finish_kernel(scaled_ref, q_ref, squares_ref, inner_ref, own_ref, far_ref, dq_ref, dk_ref):
    inverse = inverse_columns(squares_ref)
    factor = inverse * inverse * inverse * to_columns(inner_ref[...]) / FEAT
    for t in range(q_ref.shape[1] // LANES):
        cols = slice(t * LANES, (t + 1) * LANES)
        x = q_ref[:, cols].astype(jnp.float32)
        dq_ref[:, cols] = (inverse * scaled_ref[:, cols] - x * factor).astype(jnp.bfloat16)
    dk_ref[...] = (own_ref[...] + far_ref[...].astype(jnp.float32)).astype(jnp.bfloat16)


def kernel_call(body, name, steps, ins, outs, scratch=(), flops=0):
    shapes = [shape for _, shape in outs]
    moved = sum(s.size * s.dtype.itemsize for s in shapes)
    return pl.pallas_call(
        body,
        grid=(steps,),
        in_specs=ins,
        out_specs=[spec for spec, _ in outs],
        out_shape=shapes,
        scratch_shapes=list(scratch),
        name=name,
        cost_estimate=pl.CostEstimate(flops=flops, bytes_accessed=2 * moved, transcendentals=0),
        compiler_params=pltpu.CompilerParams(
            dimension_semantics=("arbitrary",), vmem_limit_bytes=32 * 1024 * 1024
        ),
    )


def local(queries, query_gain, keys, values, neighbours, d_out):
    rows, width = queries.shape
    heads = width // HS
    groups = rows // GROUP
    steps = width // WIDE
    count = lax.axis_size("dp")
    go, come, across = out_and_back(count)
    place = jnp.full((1,), lax.axis_index("dp"), jnp.int32)
    gain = query_gain[None, :]

    scalars = pl.BlockSpec(memory_space=pltpu.SMEM)
    slot = pl.BlockSpec((GROUP, WIDE), lambda i: (0, i))
    tall = pl.BlockSpec((rows, WIDE), lambda i: (0, i))
    line = pl.BlockSpec((1, WIDE), lambda i: (0, i))
    row = pl.BlockSpec((1, rows), lambda i: (0, 0))
    stat = pl.BlockSpec((CHUNK, LANES), lambda i: (i, 0))
    stat_whole = pl.BlockSpec((heads, LANES), lambda i: (0, 0))
    slot_out = (slot, jax.ShapeDtypeStruct((GROUP, width), jnp.bfloat16))
    tall_out = (tall, jax.ShapeDtypeStruct((rows, width), jnp.bfloat16))
    tall_wide = (tall, jax.ShapeDtypeStruct((rows, width), jnp.float32))
    row_out = (row, jax.ShapeDtypeStruct((1, rows), jnp.float32))
    stat_shape = jax.ShapeDtypeStruct((heads, LANES), jnp.float32)
    stat_out, stat_whole_out = (stat, stat_shape), (stat_whole, stat_shape)
    totals = pltpu.VMEM((rows, LANES), jnp.float32)
    product = 2 * SLOTS * GROUP * keys.shape[0] * width

    def with_place(kernel):
        return functools.partial(kernel, count, groups)

    far_keys = across(keys)
    *g_parts, squares = kernel_call(
        with_place(prepare_grads_kernel), "prepare_grads", steps,
        [scalars] * 2 + [tall] * 2, [slot_out] * SLOTS + [row_out], [totals],
    )(place, neighbours, d_out, queries)
    squares = lax.psum(squares, "mp")
    q_parts = kernel_call(
        with_place(prepare_queries_kernel), "prepare_queries", steps,
        [scalars] * 2 + [tall, line, row], [slot_out] * SLOTS,
        [pltpu.VMEM((rows, WIDE), jnp.bfloat16)],
    )(place, neighbours, queries, gain, squares)
    q_slots = go(q_parts)
    far_values = across(values)
    g_slots = go(g_parts)

    stats = kernel_call(
        scores_kernel, "scores", steps, [slot] * SLOTS + [tall] * 2, [stat_out] * SLOTS,
        flops=product,
    )(*q_slots, keys, far_keys)
    back = kernel_call(
        with_place(combine_scores_kernel), "combine_scores", 1,
        [scalars] * 2 + [stat_whole] * SLOTS, [stat_whole_out] * SLOTS,
    )(place, neighbours, *come(stats))
    back = go(back)

    *outs, own_dv, far_dv = kernel_call(
        context_kernel, "context", steps,
        [slot] * (2 * SLOTS) + [stat] * SLOTS + [tall] * 4,
        [slot_out] * SLOTS + [stat_out] * SLOTS + [tall_wide, tall_out],
        flops=4 * product,
    )(*q_slots, *g_slots, *back, keys, far_keys, values, far_values)
    contexts, centres = outs[:SLOTS], outs[SLOTS:]
    centres = kernel_call(
        with_place(combine_centres_kernel), "combine_centres", 1,
        [scalars] * 2 + [stat_whole] * SLOTS, [stat_whole_out] * SLOTS,
    )(place, neighbours, *come(centres))
    centres = go(centres)
    far_dv = across(far_dv)
    contexts = come(contexts)

    *grads, own_dk, far_dk = kernel_call(
        gradient_kernel, "gradient", steps,
        [slot] * (2 * SLOTS) + [stat] * (2 * SLOTS) + [tall] * 4,
        [slot_out] * SLOTS + [tall_wide, tall_out],
        flops=4 * product,
    )(*q_slots, *g_slots, *back, *centres, keys, far_keys, values, far_values)
    far_dk = across(far_dk)
    grads = come(grads)

    attended, d_values = kernel_call(
        with_place(attended_kernel), "attended", steps,
        [scalars] * 2 + [slot] * SLOTS + [tall] * 2, [tall_out] * 2,
    )(place, neighbours, *contexts, own_dv, far_dv)
    scaled, inner = kernel_call(
        with_place(inner_kernel), "inner", steps,
        [scalars] * 2 + [slot] * SLOTS + [tall, line], [tall_wide, row_out], [totals],
    )(place, neighbours, *grads, queries, gain)
    inner = lax.psum(inner, "mp")
    d_queries, d_keys = kernel_call(
        finish_kernel, "finish", steps, [tall, tall, row, row, tall, tall], [tall_out] * 2,
    )(scaled, queries, squares, inner, own_dk, far_dk)
    return (attended, d_queries, d_keys, d_values)


def solution(mesh):
    placed = (P("dp", "mp"), P("mp"), P("dp", "mp"), P("dp", "mp"), P("dp", None), P("dp", "mp"))
    return jax.shard_map(
        local,
        mesh=mesh,
        in_specs=placed,
        out_specs=(P("dp", "mp"), P("dp", "mp"), P("dp", "mp"), P("dp", "mp")),
        check_vma=False,
    )
```

```python
import functools

import jax
import jax.numpy as jnp
from jax import lax
from jax.experimental import pallas as pl
from jax.experimental.pallas import tpu as pltpu
from jax.sharding import PartitionSpec as P

HEADS = 64
HS = 128
GROUP = 64
FEAT = HEADS * HS
EPSILON = 1e-06
SCALING = 1.0 / HS**0.5
LANES = 128
CHUNK = 8
VMEM_LIMIT = 16 * 1024 * 1024
SLOTS = 5
OWN = (0, 2)
PARTNER = (1, 3, 4)


def routes(count):
    def side(i):
        return -4 if i & 2 == 0 else 4

    diagonal = (-3, -1, 1, 3)
    return {
        "y": [(i, i ^ 2) for i in range(count)],
        2: [(i, i ^ 1) for i in range(count)],
        3: [(i, (i + side(i)) % count) for i in range(count)],
        4: [(i, (i + diagonal[i & 3]) % count) for i in range(count)],
    }


def sent(array, route):
    return lax.ppermute(array, "dp", route)


def out_and_back(count):
    route = routes(count)
    back = {s: [(b, a) for a, b in route[s]] for s in (2, 3, 4)}

    return route, back, functools.partial(sent, route=route["y"])


def dot(a, b, left, right):
    return lax.dot_general(a, b, (((left,), (right,)), ((), ())), preferred_element_type=jnp.float32)


def group_numbers(place_ref, near_ref, count, groups):
    place = place_ref[0]
    one = 1 - 2 * (place & 1)
    two = 2 - 2 * (place & 2)
    numbers = []
    for offset in (0, two, one, -two, -one):
        block = lax.rem(place + offset + count, count)
        number = jnp.int32(-1)
        for g in range(groups):
            used = (near_ref[g, 0] == block) | (near_ref[g, 1] == block)
            number = jnp.where(used, g, number)
        numbers.append(number)
    return numbers


def rows_of(number):
    return pl.ds(pl.multiple_of(jnp.maximum(number, 0) * GROUP, GROUP), GROUP)


def to_row(x):
    return jnp.sum(x.T, axis=0, keepdims=True)


def to_columns(row):
    return jnp.broadcast_to(row, (row.shape[1], row.shape[1])).T


def tile(t):
    return slice(t * LANES, (t + 1) * LANES)


def squares_kernel(q_ref, squares_ref):
    x = q_ref[:, tile(0)].astype(jnp.float32)
    total = x * x
    for t in range(1, q_ref.shape[1] // LANES):
        x = q_ref[:, tile(t)].astype(jnp.float32)
        total = total + x * x
    squares_ref[...] = to_row(total)


def prepare_grads_kernel(count, groups, place_ref, near_ref, g_ref, *slot_refs):
    numbers = group_numbers(place_ref, near_ref, count, groups)
    for s in range(SLOTS):
        slot_refs[s][...] = g_ref[rows_of(numbers[s])]


def inverse_columns(squares_ref):
    return to_columns(lax.rsqrt(squares_ref[...] / FEAT + EPSILON))


def prepare_queries_kernel(count, groups, place_ref, near_ref, q_ref, gain_ref, squares_ref, *refs):
    slot_refs, normed_ref = refs[:SLOTS], refs[SLOTS]
    numbers = group_numbers(place_ref, near_ref, count, groups)
    inverse = inverse_columns(squares_ref)
    for t in range(q_ref.shape[1] // LANES):
        x = q_ref[:, tile(t)].astype(jnp.float32)
        normed_ref[:, tile(t)] = (x * gain_ref[:, tile(t)] * inverse).astype(jnp.bfloat16)
    for s in range(SLOTS):
        slot_refs[s][...] = normed_ref[rows_of(numbers[s])]


def head(refs, slots, cols):
    return jnp.concatenate([refs[s][:, cols] for s in slots], axis=0)


def each_chunk(heads, unit, body):
    def step(i, carry):
        first = i * unit
        cols = [pl.ds(pl.multiple_of((first + h) * HS, HS), HS) for h in range(unit)]
        body(pl.ds(pl.multiple_of(first, unit), unit), cols)
        return carry

    lax.fori_loop(0, heads // unit, step, 0)


def scores_kernel(*refs):
    q_refs, k_refs, stat_refs = refs[:SLOTS], refs[SLOTS : SLOTS + 2], refs[SLOTS + 2 :]

    def body(rows, cols):
        for slots, k_ref in zip((OWN, PARTNER), k_refs):
            scores = [dot(k_ref[:, c], head(q_refs, slots, c), 1, 1) * SCALING for c in cols]
            tops = [jnp.max(x, axis=0, keepdims=True) for x in scores]
            totals = [
                jnp.sum(jnp.exp(x - top), axis=0, keepdims=True) for x, top in zip(scores, tops)
            ]
            tops = jnp.concatenate(tops, axis=0)
            totals = jnp.concatenate(totals, axis=0)
            for at, s in enumerate(slots):
                lanes = slice(at * GROUP, (at + 1) * GROUP)
                stat_refs[s][rows] = jnp.concatenate([tops[:, lanes], totals[:, lanes]], axis=1)

    each_chunk(stat_refs[0].shape[0], CHUNK, body)


def combine_scores_kernel(count, groups, place_ref, near_ref, *refs):
    stat_refs, back_refs = refs[:SLOTS], refs[SLOTS:]
    numbers = group_numbers(place_ref, near_ref, count, groups)
    heads = stat_refs[0].shape[0]
    shape = (heads, GROUP)
    tops = [r[:, 0:GROUP] for r in stat_refs]
    totals = [r[:, GROUP : 2 * GROUP] for r in stat_refs]
    number_of = [jnp.full(shape, n, jnp.int32) for n in numbers]
    lowest = jnp.full(shape, -jnp.inf, jnp.float32)
    zero = jnp.zeros(shape, jnp.float32)
    merged = []
    for g in range(groups):
        top, total = lowest, zero
        for s in range(SLOTS):
            top = jnp.maximum(top, jnp.where(number_of[s] == g, tops[s], lowest))
        for s in range(SLOTS):
            mine = number_of[s] == g
            factor = jnp.exp(jnp.where(mine, tops[s] - top, zero))
            total = total + jnp.where(mine, totals[s] * factor, zero)
        merged.append((top, 1.0 / total))
    for s in range(SLOTS):
        top, inv = tops[s], zero
        for g in range(groups):
            mine = number_of[s] == g
            top = jnp.where(mine, merged[g][0], top)
            inv = jnp.where(mine, merged[g][1], inv)
        back_refs[s][...] = jnp.concatenate([top, inv], axis=1)


def combine_centres_kernel(count, groups, place_ref, near_ref, *refs):
    stat_refs, back_refs = refs[:SLOTS], refs[SLOTS:]
    numbers = group_numbers(place_ref, near_ref, count, groups)
    shape = stat_refs[0].shape
    number_of = [jnp.full(shape, n, jnp.int32) for n in numbers]
    zero = jnp.zeros(shape, jnp.float32)
    totals = []
    for g in range(groups):
        total = zero
        for s in range(SLOTS):
            total = total + jnp.where(number_of[s] == g, stat_refs[s][...], zero)
        totals.append(total)
    for s in range(SLOTS):
        here = zero
        for g in range(groups):
            here = jnp.where(number_of[s] == g, totals[g], here)
        back_refs[s][...] = here


def stat_rows(stat_refs, slots, rows, half):
    lanes = slice(half * GROUP, (half + 1) * GROUP)
    return jnp.concatenate([stat_refs[s][rows, lanes] for s in slots], axis=1)


def units(rows, slots, back_refs, q_refs, k_ref, cols):
    top, inv = stat_rows(back_refs, slots, rows, 0), stat_rows(back_refs, slots, rows, 1)
    scores = [dot(k_ref[:, c], head(q_refs, slots, c), 1, 1) for c in cols]
    return [
        jnp.exp(x * SCALING - top[h : h + 1]) * inv[h : h + 1] for h, x in enumerate(scores)
    ]


def context_kernel(*refs):
    q_refs, g_refs, back_refs = (refs[i * SLOTS : (i + 1) * SLOTS] for i in range(3))
    k_refs, v_refs = refs[3 * SLOTS : 3 * SLOTS + 2], refs[3 * SLOTS + 2 : 3 * SLOTS + 4]
    rest = refs[3 * SLOTS + 4 :]
    ctx_refs, centre_refs, dv_ref = rest[:SLOTS], rest[SLOTS : 2 * SLOTS], rest[2 * SLOTS]

    def body(rows, cols):
        work = []
        for slots, k_ref, v_ref in zip((OWN, PARTNER), k_refs, v_refs):
            probs = units(rows, slots, back_refs, q_refs, k_ref, cols)
            work.append((slots, v_ref, probs))
        for slots, v_ref, probs in work:
            centres = []
            for c, p in zip(cols, probs):
                low, g, v = p.astype(jnp.bfloat16), head(g_refs, slots, c), v_ref[:, c]
                context = dot(low, v, 0, 0).astype(jnp.bfloat16)
                for at, s in enumerate(slots):
                    ctx_refs[s][:, c] = context[at * GROUP : (at + 1) * GROUP]
                centres.append(jnp.sum(p * dot(v, g, 1, 1), axis=0, keepdims=True))
                if slots is PARTNER:
                    dv_ref[:, c] = dot(low, g, 1, 0).astype(jnp.bfloat16)
            centres = jnp.concatenate(centres, axis=0)
            empty = jnp.zeros((centres.shape[0], GROUP), jnp.float32)
            for at, s in enumerate(slots):
                lanes = slice(at * GROUP, (at + 1) * GROUP)
                centre_refs[s][rows] = jnp.concatenate([centres[:, lanes], empty], axis=1)

    each_chunk(centre_refs[0].shape[0], CHUNK, body)


def gradient_kernel(*refs):
    q_refs, g_refs, back_refs, centre_refs = (refs[i * SLOTS : (i + 1) * SLOTS] for i in range(4))
    k_refs, v_refs = refs[4 * SLOTS : 4 * SLOTS + 2], refs[4 * SLOTS + 2 : 4 * SLOTS + 4]
    rest = refs[4 * SLOTS + 4 :]
    grad_refs, dk_ref = rest[:SLOTS], rest[SLOTS]

    def body(rows, cols):
        work = []
        for slots, k_ref, v_ref in zip((OWN, PARTNER), k_refs, v_refs):
            probs = units(rows, slots, back_refs, q_refs, k_ref, cols)
            centre = stat_rows(centre_refs, slots, rows, 0)
            products = [dot(v_ref[:, c], head(g_refs, slots, c), 1, 1) for c in cols]
            lows = [
                (p * (x - centre[h : h + 1])).astype(jnp.bfloat16)
                for h, (p, x) in enumerate(zip(probs, products))
            ]
            work.append((slots, k_ref, lows))
        for slots, k_ref, lows in work:
            for c, low in zip(cols, lows):
                grad = (dot(low, k_ref[:, c], 0, 0) * SCALING).astype(jnp.bfloat16)
                for at, s in enumerate(slots):
                    grad_refs[s][:, c] = grad[at * GROUP : (at + 1) * GROUP]
                if slots is PARTNER:
                    product = dot(low, head(q_refs, slots, c), 1, 0) * SCALING
                    dk_ref[:, c] = product.astype(jnp.bfloat16)

    each_chunk(back_refs[0].shape[0], CHUNK, body)


def own_kernel(*refs):
    pairs = [dict(zip(OWN, refs[i * 2 : i * 2 + 2])) for i in range(4)]
    q_refs, g_refs, back_refs, centre_refs = pairs
    k_ref, v_ref, far_ref, dv_ref, dk_ref = refs[8:]

    def body(rows, cols):
        probs = units(rows, OWN, back_refs, q_refs, k_ref, cols)
        centre = stat_rows(centre_refs, OWN, rows, 0)
        grads = [head(g_refs, OWN, c) for c in cols]
        products = [dot(v_ref[:, c], g, 1, 1) for c, g in zip(cols, grads)]
        for h, (c, p, g, x) in enumerate(zip(cols, probs, grads, products)):
            total = dot(p.astype(jnp.bfloat16), g, 1, 0) + far_ref[:, c].astype(jnp.float32)
            dv_ref[:, c] = total.astype(jnp.bfloat16)
            low = (p * (x - centre[h : h + 1])).astype(jnp.bfloat16)
            dk_ref[:, c] = dot(low, head(q_refs, OWN, c), 1, 0) * SCALING

    each_chunk(back_refs[0].shape[0], CHUNK, body)


def gathered(weights, refs, t):
    total = None
    for s in range(SLOTS):
        part = weights[s] * refs[s][:, tile(t)].astype(jnp.float32)
        total = part if total is None else total + part
    return total


def weights_of(numbers, g):
    return [jnp.where(n == g, 1.0, 0.0) for n in numbers]


def attended_kernel(count, groups, place_ref, near_ref, *refs):
    ctx_refs, out_ref = refs[:SLOTS], refs[SLOTS]
    numbers = group_numbers(place_ref, near_ref, count, groups)
    for g in range(groups):
        weights = weights_of(numbers, g)
        rows = slice(g * GROUP, (g + 1) * GROUP)
        for t in range(out_ref.shape[1] // LANES):
            out_ref[rows, tile(t)] = gathered(weights, ctx_refs, t).astype(jnp.bfloat16)


def inner_kernel(count, groups, place_ref, near_ref, *refs):
    grad_refs = refs[:SLOTS]
    q_ref, gain_ref, scaled_ref, inner_ref = refs[SLOTS:]
    numbers = group_numbers(place_ref, near_ref, count, groups)
    totals = []
    for g in range(groups):
        weights = weights_of(numbers, g)
        rows = slice(g * GROUP, (g + 1) * GROUP)
        total = jnp.zeros((GROUP, LANES), jnp.float32)
        for t in range(q_ref.shape[1] // LANES):
            scaled = gathered(weights, grad_refs, t) * gain_ref[:, tile(t)]
            scaled_ref[rows, tile(t)] = scaled
            total = total + scaled * q_ref[rows, tile(t)].astype(jnp.float32)
        totals.append(total)
    inner_ref[...] = to_row(jnp.concatenate(totals, axis=0))


def finish_kernel(scaled_ref, q_ref, squares_ref, inner_ref, dq_ref):
    inverse = inverse_columns(squares_ref)
    factor = inverse * inverse * inverse * to_columns(inner_ref[...]) / FEAT
    for t in range(q_ref.shape[1] // LANES):
        x = q_ref[:, tile(t)].astype(jnp.float32)
        dq_ref[:, tile(t)] = (inverse * scaled_ref[:, tile(t)] - x * factor).astype(jnp.bfloat16)


def in_vmem(array):
    return pltpu.with_memory_space_constraint(array, pltpu.VMEM)


def after(values, *tokens):
    return lax.optimization_barrier((values, tokens))[0]


def kernel_call(body, name, outs, scratch=(), scalars=0, last=()):
    vmem = pl.BlockSpec(memory_space=pltpu.VMEM)

    def call(*args):
        small, large = args[:scalars], [in_vmem(a) for a in args[scalars:]]
        shapes = [
            (jax.ShapeDtypeStruct if i in last else pltpu.VMEM)(shape, dtype)
            for i, (shape, dtype) in enumerate(outs)
        ]
        results = pl.pallas_call(
            body,
            in_specs=[pl.BlockSpec(memory_space=pltpu.SMEM)] * scalars + [vmem] * len(large),
            out_specs=[vmem] * len(outs),
            out_shape=shapes,
            scratch_shapes=list(scratch),
            name=name,
            cost_estimate=pl.CostEstimate(flops=0, bytes_accessed=0, transcendentals=0),
            compiler_params=pltpu.CompilerParams(vmem_limit_bytes=VMEM_LIMIT),
        )(*small, *large)
        return list(results)

    return call


def local(queries, query_gain, keys, values, neighbours, d_out):
    rows, width = queries.shape
    heads = width // HS
    groups = rows // GROUP
    count = lax.axis_size("dp")
    route, back_route, across = out_and_back(count)
    place = jnp.full((1,), lax.axis_index("dp"), jnp.int32)
    gain = query_gain[None, :]

    slot = ((GROUP, width), jnp.bfloat16)
    tall = ((rows, width), jnp.bfloat16)
    tall_wide = ((rows, width), jnp.float32)
    row = ((1, rows), jnp.float32)
    stat = ((heads, LANES), jnp.float32)

    def go(parts):
        return [sent(p, route[s]) if s >= 2 else p for s, p in enumerate(parts)]

    def come(parts):
        return [sent(p, back_route[s]) if s >= 2 else p for s, p in enumerate(parts)]

    def placed(kernel, name, outs, scratch=(), last=()):
        call = kernel_call(
            functools.partial(kernel, count, groups), name, outs, scratch, 2, last
        )
        return functools.partial(call, place, neighbours)

    far_keys = across(keys)
    far_values = across(values)
    (squares,) = kernel_call(squares_kernel, "squares", [row])(queries)
    squares = lax.psum(squares, "mp")
    q_parts = placed(
        prepare_queries_kernel, "prepare_queries", [slot] * SLOTS, [pltpu.VMEM(*tall)]
    )(queries, gain, squares)
    q_slots = go(q_parts)
    g_parts = placed(prepare_grads_kernel, "prepare_grads", [slot] * SLOTS)(
        after(d_out, q_parts[0])
    )

    stats = kernel_call(scores_kernel, "scores", [stat] * SLOTS)(*q_slots, keys, far_keys)
    stats = come(stats)
    g_parts[4] = after(g_parts[4], *stats[2:])
    g_slots = go(g_parts)
    back = placed(combine_scores_kernel, "combine_scores", [stat] * SLOTS)(*stats)
    back = go(back)

    *outs, far_dv = kernel_call(
        context_kernel, "context", [slot] * SLOTS + [stat] * SLOTS + [tall]
    )(*q_slots, *g_slots, *back, keys, far_keys, values, far_values)
    contexts, centres = outs[:SLOTS], outs[SLOTS:]
    centres = come(centres)
    far_dv = across(far_dv)
    centres = placed(combine_centres_kernel, "combine_centres", [stat] * SLOTS)(*centres)
    centres = go(centres)
    contexts[4] = after(contexts[4], *centres[2:])
    contexts = come(contexts)

    *grads, far_dk = kernel_call(gradient_kernel, "gradient", [slot] * SLOTS + [tall])(
        *q_slots, *g_slots, *back, *centres, keys, far_keys, values, far_values
    )
    own = [part[s] for part in (q_slots, g_slots, back, centres) for s in OWN]
    own[0] = after(own[0], far_dk)
    far_dk = across(far_dk)
    grads = come(grads)

    d_values, own_dk = kernel_call(own_kernel, "own", [tall, tall_wide], last=(0,))(
        *own, keys, values, far_dv
    )
    (attended,) = placed(attended_kernel, "attended", [tall], last=(0,))(*contexts)
    grads = after(grads, attended, d_values)
    scaled, inner = placed(inner_kernel, "inner", [tall_wide, row])(*grads, queries, gain)
    inner = lax.psum(inner, "mp")
    (d_queries,) = kernel_call(finish_kernel, "finish", [tall], last=(0,))(
        scaled, queries, squares, inner
    )
    d_keys = (own_dk + far_dk.astype(jnp.float32)).astype(jnp.bfloat16)
    return (attended, d_queries, d_keys, d_values)


def solution(mesh):
    placed = (P("dp", "mp"), P("mp"), P("dp", "mp"), P("dp", "mp"), P("dp", None), P("dp", "mp"))
    return jax.shard_map(
        local,
        mesh=mesh,
        in_specs=placed,
        out_specs=(P("dp", "mp"), P("dp", "mp"), P("dp", "mp"), P("dp", "mp")),
        check_vma=False,
    )
```

```python
import functools

import jax
import jax.numpy as jnp
from jax import lax
from jax.experimental import pallas as pl
from jax.experimental.pallas import tpu as pltpu
from jax.sharding import PartitionSpec as P

HEADS = 64
HS = 128
GROUP = 64
FEAT = HEADS * HS
EPSILON = 1e-06
SCALING = 1.0 / HS**0.5
LANES = 128
CHUNK = 8
VMEM_LIMIT = 8 * 1024 * 1024
WORK = 8 * 1024 * 1024
SLOTS = 5
OWN = (0, 2)
PARTNER = (1, 3, 4)


def routes(count):
    def side(i):
        return -4 if i & 2 == 0 else 4

    diagonal = (-3, -1, 1, 3)
    return {
        "y": [(i, i ^ 2) for i in range(count)],
        2: [(i, i ^ 1) for i in range(count)],
        3: [(i, (i + side(i)) % count) for i in range(count)],
        4: [(i, (i + diagonal[i & 3]) % count) for i in range(count)],
    }


def sent(array, route):
    return lax.ppermute(array, "dp", route)


def out_and_back(count):
    route = routes(count)
    back = {s: [(b, a) for a, b in route[s]] for s in (2, 3, 4)}

    return route, back, functools.partial(sent, route=route["y"])


def dot(a, b, left, right):
    return lax.dot_general(a, b, (((left,), (right,)), ((), ())), preferred_element_type=jnp.float32)


def group_numbers(place_ref, near_ref, count, groups):
    place = place_ref[0]
    one = 1 - 2 * (place & 1)
    two = 2 - 2 * (place & 2)
    numbers = []
    for offset in (0, two, one, -two, -one):
        block = lax.rem(place + offset + count, count)
        number = jnp.int32(-1)
        for g in range(groups):
            used = (near_ref[g, 0] == block) | (near_ref[g, 1] == block)
            number = jnp.where(used, g, number)
        numbers.append(number)
    return numbers


def rows_of(number):
    return pl.ds(pl.multiple_of(jnp.maximum(number, 0) * GROUP, GROUP), GROUP)


def to_row(x):
    return jnp.sum(x.T, axis=0, keepdims=True)


def to_columns(row):
    return jnp.broadcast_to(row, (row.shape[1], row.shape[1])).T


def tile(t):
    return slice(t * LANES, (t + 1) * LANES)


def squares_kernel(q_ref, squares_ref):
    x = q_ref[:, tile(0)].astype(jnp.float32)
    total = x * x
    for t in range(1, q_ref.shape[1] // LANES):
        x = q_ref[:, tile(t)].astype(jnp.float32)
        total = total + x * x
    squares_ref[...] = to_row(total)


def pick_kernel(slots, count, groups, place_ref, near_ref, g_ref, *slot_refs):
    numbers = group_numbers(place_ref, near_ref, count, groups)
    for s, slot_ref in zip(slots, slot_refs):
        slot_ref[...] = g_ref[rows_of(numbers[s])]


def added(refs):
    total = refs[0][...]
    for ref in refs[1:]:
        total = total + ref[...]
    return total


def inverse_columns(squares_refs):
    return to_columns(lax.rsqrt(added(squares_refs) / FEAT + EPSILON))


def prepare_queries_kernel(count, groups, place_ref, near_ref, q_ref, gain_ref, *refs):
    *squares_refs, normed_ref, _, _, _ = refs
    slot_refs = refs[-3:]
    numbers = group_numbers(place_ref, near_ref, count, groups)
    inverse = inverse_columns(squares_refs)
    for t in range(q_ref.shape[1] // LANES):
        x = q_ref[:, tile(t)].astype(jnp.float32)
        normed_ref[:, tile(t)] = (x * gain_ref[:, tile(t)] * inverse).astype(jnp.bfloat16)
    for slot_ref, number in zip(slot_refs, numbers[2:]):
        slot_ref[...] = normed_ref[rows_of(number)]


def slot_views(numbers, whole_ref, slot_refs):
    own = [whole_ref.at[rows_of(numbers[s])] for s in range(SLOTS - len(slot_refs))]
    return own + list(slot_refs)


def head(refs, slots, cols):
    return jnp.concatenate([refs[s][:, cols] for s in slots], axis=0)


def each_chunk(heads, unit, body):
    def step(i, carry):
        first = i * unit
        cols = [pl.ds(pl.multiple_of((first + h) * HS, HS), HS) for h in range(unit)]
        body(pl.ds(pl.multiple_of(first, unit), unit), cols)
        return carry

    lax.fori_loop(0, heads // unit, step, 0)


def scores_kernel(count, groups, place_ref, near_ref, *refs):
    numbers = group_numbers(place_ref, near_ref, count, groups)
    q_refs = slot_views(numbers, refs[0], refs[1:4])
    k_refs, stat_refs, weight_refs = refs[4:6], refs[6 : 6 + SLOTS], refs[6 + SLOTS :]

    def body(rows, cols):
        for slots, k_ref, weight_ref in zip((OWN, PARTNER), k_refs, weight_refs):
            scores = [dot(k_ref[:, c], head(q_refs, slots, c), 1, 1) * SCALING for c in cols]
            tops = [jnp.max(x, axis=0, keepdims=True) for x in scores]
            totals = []
            for c, x, top in zip(cols, scores, tops):
                weights = jnp.exp(x - top)
                weight_ref[c] = weights
                totals.append(jnp.sum(weights, axis=0, keepdims=True))
            tops = jnp.concatenate(tops, axis=0)
            totals = jnp.concatenate(totals, axis=0)
            for at, s in enumerate(slots):
                lanes = slice(at * GROUP, (at + 1) * GROUP)
                stat_refs[s][rows] = jnp.concatenate([tops[:, lanes], totals[:, lanes]], axis=1)

    each_chunk(stat_refs[0].shape[0], CHUNK, body)


def combine_scores_kernel(count, groups, place_ref, near_ref, *refs):
    stat_refs, back_refs = refs[:SLOTS], refs[SLOTS:]
    numbers = group_numbers(place_ref, near_ref, count, groups)
    heads = stat_refs[0].shape[0]
    shape = (heads, GROUP)
    tops = [r[:, 0:GROUP] for r in stat_refs]
    totals = [r[:, GROUP : 2 * GROUP] for r in stat_refs]
    number_of = [jnp.full(shape, n, jnp.int32) for n in numbers]
    lowest = jnp.full(shape, -jnp.inf, jnp.float32)
    zero = jnp.zeros(shape, jnp.float32)
    merged = []
    for g in range(groups):
        top, total = lowest, zero
        for s in range(SLOTS):
            top = jnp.maximum(top, jnp.where(number_of[s] == g, tops[s], lowest))
        for s in range(SLOTS):
            mine = number_of[s] == g
            factor = jnp.exp(jnp.where(mine, tops[s] - top, zero))
            total = total + jnp.where(mine, totals[s] * factor, zero)
        merged.append((top, 1.0 / total))
    for s in range(SLOTS):
        share = zero
        for g in range(groups):
            mine = number_of[s] == g
            factor = jnp.exp(jnp.where(mine, tops[s] - merged[g][0], zero))
            share = jnp.where(mine, factor * merged[g][1], share)
        back_refs[s][...] = jnp.concatenate([share, zero], axis=1)


def combine_centres_kernel(count, groups, place_ref, near_ref, *refs):
    stat_refs, back_refs = refs[:SLOTS], refs[SLOTS:]
    numbers = group_numbers(place_ref, near_ref, count, groups)
    shape = stat_refs[0].shape
    number_of = [jnp.full(shape, n, jnp.int32) for n in numbers]
    zero = jnp.zeros(shape, jnp.float32)
    totals = []
    for g in range(groups):
        total = zero
        for s in range(SLOTS):
            total = total + jnp.where(number_of[s] == g, stat_refs[s][...], zero)
        totals.append(total)
    for s in range(SLOTS):
        here = zero
        for g in range(groups):
            here = jnp.where(number_of[s] == g, totals[g], here)
        back_refs[s][...] = here


def stat_rows(stat_refs, slots, rows):
    return jnp.concatenate([stat_refs[s][rows, 0:GROUP] for s in slots], axis=1)


def probs_of(rows, slots, back_refs, weight_ref, cols):
    shares = stat_rows(back_refs, slots, rows)
    return [weight_ref[c] * shares[h : h + 1] for h, c in enumerate(cols)]


def centres_kernel(count, groups, place_ref, near_ref, *refs):
    numbers = group_numbers(place_ref, near_ref, count, groups)
    g_refs = slot_views(numbers, refs[0], refs[1:4])
    v_refs, weight_refs, back_refs = refs[4:6], refs[6:8], refs[8 : 8 + SLOTS]
    centre_refs = refs[8 + SLOTS : 8 + 2 * SLOTS]
    *product_refs, dv_ref = refs[8 + 2 * SLOTS :]

    def body(rows, cols):
        for slots, v_ref, weight_ref, product_ref in zip(
            (OWN, PARTNER), v_refs, weight_refs, product_refs
        ):
            products = [dot(v_ref[:, c], head(g_refs, slots, c), 1, 1) for c in cols]
            probs = probs_of(rows, slots, back_refs, weight_ref, cols)
            for c, x, p in zip(cols, products, probs):
                product_ref[c] = x
                if slots is PARTNER:
                    product = dot(p.astype(jnp.bfloat16), head(g_refs, slots, c), 1, 0)
                    dv_ref[:, c] = product.astype(jnp.bfloat16)
            centres = [jnp.sum(p * x, axis=0, keepdims=True) for p, x in zip(probs, products)]
            centres = jnp.concatenate(centres, axis=0)
            empty = jnp.zeros((centres.shape[0], GROUP), jnp.float32)
            for at, s in enumerate(slots):
                lanes = slice(at * GROUP, (at + 1) * GROUP)
                centre_refs[s][rows] = jnp.concatenate([centres[:, lanes], empty], axis=1)

    each_chunk(centre_refs[0].shape[0], CHUNK, body)


def context_kernel(*refs):
    v_refs, weight_refs, back_refs = refs[0:2], refs[2:4], refs[4 : 4 + SLOTS]
    ctx_refs = refs[4 + SLOTS :]

    def body(rows, cols):
        for slots, v_ref, weight_ref in zip((OWN, PARTNER), v_refs, weight_refs):
            probs = probs_of(rows, slots, back_refs, weight_ref, cols)
            for c, p in zip(cols, probs):
                context = dot(p.astype(jnp.bfloat16), v_ref[:, c], 0, 0).astype(jnp.bfloat16)
                for at, s in enumerate(slots):
                    ctx_refs[s][:, c] = context[at * GROUP : (at + 1) * GROUP]

    each_chunk(back_refs[0].shape[0], CHUNK, body)


def grad_scores_of(rows, slots, back_refs, centre_refs, weight_ref, product_ref, cols):
    probs = probs_of(rows, slots, back_refs, weight_ref, cols)
    centre = stat_rows(centre_refs, slots, rows)
    return probs, [
        (p * (product_ref[c] - centre[h : h + 1])).astype(jnp.bfloat16)
        for h, (c, p) in enumerate(zip(cols, probs))
    ]


def gradient_kernel(count, groups, place_ref, near_ref, *refs):
    numbers = group_numbers(place_ref, near_ref, count, groups)
    q_refs = slot_views(numbers, refs[0], refs[1:4])
    k_refs, weight_refs, product_refs, rest = refs[4:6], refs[6:8], refs[8:10], refs[10:]
    back_refs, centre_refs, grad_refs = (rest[i * SLOTS : (i + 1) * SLOTS] for i in range(3))
    dk_ref = rest[3 * SLOTS]

    def body(rows, cols):
        for slots, k_ref, weight_ref, product_ref in zip(
            (OWN, PARTNER), k_refs, weight_refs, product_refs
        ):
            _, lows = grad_scores_of(
                rows, slots, back_refs, centre_refs, weight_ref, product_ref, cols
            )
            for c, low in zip(cols, lows):
                grad = (dot(low, k_ref[:, c], 0, 0) * SCALING).astype(jnp.bfloat16)
                for at, s in enumerate(slots):
                    grad_refs[s][:, c] = grad[at * GROUP : (at + 1) * GROUP]
                if slots is PARTNER:
                    product = dot(low, head(q_refs, slots, c), 1, 0) * SCALING
                    dk_ref[:, c] = product.astype(jnp.bfloat16)

    each_chunk(back_refs[0].shape[0], CHUNK, body)


def own_kernel(count, groups, place_ref, near_ref, *refs):
    numbers = group_numbers(place_ref, near_ref, count, groups)
    normed_ref, q_ref, grad_ref, g_ref, weight_ref, product_ref = refs[:6]
    q_refs = dict(zip(OWN, (normed_ref.at[rows_of(numbers[0])], q_ref)))
    g_refs = dict(zip(OWN, (grad_ref.at[rows_of(numbers[0])], g_ref)))
    back_refs, centre_refs = dict(zip(OWN, refs[6:8])), dict(zip(OWN, refs[8:10]))
    far_dv_ref, far_dk_ref, dv_ref, dk_ref = refs[10:]

    def body(rows, cols):
        probs, lows = grad_scores_of(
            rows, OWN, back_refs, centre_refs, weight_ref, product_ref, cols
        )
        for c, p, low in zip(cols, probs, lows):
            total = dot(p.astype(jnp.bfloat16), head(g_refs, OWN, c), 1, 0)
            total = total + far_dv_ref[:, c].astype(jnp.float32)
            dv_ref[:, c] = total.astype(jnp.bfloat16)
            total = dot(low, head(q_refs, OWN, c), 1, 0) * SCALING
            total = total + far_dk_ref[:, c].astype(jnp.float32)
            dk_ref[:, c] = total.astype(jnp.bfloat16)

    each_chunk(refs[6].shape[0], CHUNK, body)


def gathered(weights, refs, t):
    total = None
    for s in range(SLOTS):
        part = weights[s] * refs[s][:, tile(t)].astype(jnp.float32)
        total = part if total is None else total + part
    return total


def weights_of(numbers, g):
    return [jnp.where(n == g, 1.0, 0.0) for n in numbers]


def attended_kernel(count, groups, place_ref, near_ref, *refs):
    ctx_refs, out_ref = refs[:SLOTS], refs[SLOTS]
    numbers = group_numbers(place_ref, near_ref, count, groups)
    for g in range(groups):
        weights = weights_of(numbers, g)
        rows = slice(g * GROUP, (g + 1) * GROUP)
        for t in range(out_ref.shape[1] // LANES):
            out_ref[rows, tile(t)] = gathered(weights, ctx_refs, t).astype(jnp.bfloat16)


def inner_kernel(count, groups, place_ref, near_ref, *refs):
    grad_refs = refs[:SLOTS]
    q_ref, gain_ref, scaled_ref, inner_ref = refs[SLOTS:]
    numbers = group_numbers(place_ref, near_ref, count, groups)
    totals = []
    for g in range(groups):
        weights = weights_of(numbers, g)
        rows = slice(g * GROUP, (g + 1) * GROUP)
        total = jnp.zeros((GROUP, LANES), jnp.float32)
        for t in range(q_ref.shape[1] // LANES):
            scaled = gathered(weights, grad_refs, t) * gain_ref[:, tile(t)]
            scaled_ref[rows, tile(t)] = scaled
            total = total + scaled * q_ref[rows, tile(t)].astype(jnp.float32)
        totals.append(total)
    inner_ref[...] = to_row(jnp.concatenate(totals, axis=0))


def finish_kernel(scaled_ref, q_ref, *refs):
    *sum_refs, dq_ref = refs
    half = len(sum_refs) // 2
    inverse = inverse_columns(sum_refs[:half])
    factor = inverse * inverse * inverse * to_columns(added(sum_refs[half:])) / FEAT
    for t in range(q_ref.shape[1] // LANES):
        x = q_ref[:, tile(t)].astype(jnp.float32)
        dq_ref[:, tile(t)] = (inverse * scaled_ref[:, tile(t)] - x * factor).astype(jnp.bfloat16)


def spread(array, axis):
    count = lax.axis_size(axis)
    shifts = [[(i, (i + k) % count) for i in range(count)] for k in range(1, count)]
    return [array] + [lax.ppermute(array, axis, shift) for shift in shifts]


def in_vmem(array):
    return pltpu.with_memory_space_constraint(array, pltpu.VMEM)


def after(values, *tokens):
    return lax.optimization_barrier((values, tokens))[0]


def kernel_call(body, name, outs, scratch=(), scalars=0, last=(), cost=0):
    vmem = pl.BlockSpec(memory_space=pltpu.VMEM)

    def call(*args):
        small, large = args[:scalars], [in_vmem(a) for a in args[scalars:]]
        shapes = [
            (jax.ShapeDtypeStruct if i in last else pltpu.VMEM)(shape, dtype)
            for i, (shape, dtype) in enumerate(outs)
        ]
        results = pl.pallas_call(
            body,
            in_specs=[pl.BlockSpec(memory_space=pltpu.SMEM)] * scalars + [vmem] * len(large),
            out_specs=[vmem] * len(outs),
            out_shape=shapes,
            scratch_shapes=list(scratch),
            name=name,
            cost_estimate=pl.CostEstimate(flops=0, bytes_accessed=cost, transcendentals=0),
            compiler_params=pltpu.CompilerParams(vmem_limit_bytes=VMEM_LIMIT),
        )(*small, *large)
        return list(results)

    return call


def local(queries, query_gain, keys, values, neighbours, d_out):
    rows, width = queries.shape
    heads = width // HS
    groups = rows // GROUP
    count = lax.axis_size("dp")
    route, back_route, across = out_and_back(count)
    place = jnp.full((1,), lax.axis_index("dp"), jnp.int32)
    gain = query_gain[None, :]

    slot = ((GROUP, width), jnp.bfloat16)
    tall = ((rows, width), jnp.bfloat16)
    row = ((1, rows), jnp.float32)
    stat = ((heads, LANES), jnp.float32)

    def out(part, s):
        return sent(part, route[s])

    def home(part, s):
        return sent(part, back_route[s])

    def go(parts):
        return [out(p, s) if s >= 2 else p for s, p in enumerate(parts)]

    def come(parts):
        return [home(p, s) if s >= 2 else p for s, p in enumerate(parts)]

    def placed(kernel, name, outs, scratch=(), last=(), cost=0):
        call = kernel_call(
            functools.partial(kernel, count, groups), name, outs, scratch, 2, last, cost
        )
        return functools.partial(call, place, neighbours)

    def picked(slots, array):
        return placed(functools.partial(pick_kernel, slots), "pick", [slot] * len(slots))(array)

    far_keys = across(keys)
    (squares,) = kernel_call(squares_kernel, "squares", [row])(queries)
    squares = spread(squares, "mp")
    normed, *q_parts = placed(
        prepare_queries_kernel, "prepare_queries", [tall] + [slot] * 3
    )(queries, gain, *squares)
    q_slots = [out(q, s) for q, s in zip(q_parts, (2, 3, 4))]
    far_values = across(values)
    g2, g3 = picked((2, 3), after(d_out, q_parts[2]))
    g2, g3 = out(g2, 2), out(g3, 3)

    own_scores = ((width, len(OWN) * GROUP), jnp.float32)
    far_scores = ((width, len(PARTNER) * GROUP), jnp.float32)
    *stats, own_weights, far_weights = placed(
        scores_kernel, "scores", [stat] * SLOTS + [own_scores, far_scores]
    )(normed, *q_slots, keys, far_keys)
    stats[2:] = after(stats[2:], g2, g3)
    stats = come(stats)
    (g4,) = picked((4,), after(d_out, *stats[2:]))
    g_slots = [g2, g3, out(g4, 4)]
    back = placed(combine_scores_kernel, "combine_scores", [stat] * SLOTS)(*stats)
    back = go(back)

    inputs = [d_out, *g_slots, values, far_values, own_weights, far_weights]
    contexts = kernel_call(context_kernel, "context", [slot] * SLOTS)(
        *inputs[-4:], after(back[0], g_slots[2]), *back[1:]
    )
    held = [after(back[0], contexts[0]), *back[1:]]
    *centres, own_products, far_products, far_dv = placed(
        centres_kernel, "centres", [stat] * SLOTS + [own_scores, far_scores, tall]
    )(*inputs, *held)
    contexts[2:4] = [home(contexts[s], s) for s in (2, 3)]
    far_dv = across(after(far_dv, contexts[2], contexts[3]))
    centres[2:] = after(centres[2:], contexts[2], contexts[3])
    centres = come(centres)
    centres = placed(combine_centres_kernel, "combine_centres", [stat] * SLOTS)(*centres)
    centres = go(centres)
    contexts[4] = home(after(contexts[4], centres[2]), 4)

    *grads, far_dk = placed(gradient_kernel, "gradient", [slot] * SLOTS + [tall])(
        normed, *q_slots, keys, far_keys, own_weights, far_weights, own_products, far_products,
        *back, *centres,
    )
    far_dk = across(after(far_dk, far_dv))
    grads[4] = after(grads[4], contexts[4])
    grads = come(grads)

    d_values, d_keys = placed(own_kernel, "own", [tall, tall], last=(0, 1))(
        normed, q_slots[0], d_out, g2, own_weights, own_products, back[0], back[2], centres[0], centres[2],
        far_dv, far_dk,
    )
    (attended,) = placed(attended_kernel, "attended", [tall], last=(0,))(*contexts)
    grads[2:] = after(grads[2:], attended, d_values)
    scaled, inner = placed(inner_kernel, "inner", [((rows, width), jnp.float32), row])(
        *grads, queries, gain
    )
    inner = spread(inner, "mp")
    (d_queries,) = kernel_call(finish_kernel, "finish", [tall], last=(0,))(
        scaled, queries, *squares, *inner
    )
    return (attended, d_queries, d_keys, d_values)


def solution(mesh):
    placed = (P("dp", "mp"), P("mp"), P("dp", "mp"), P("dp", "mp"), P("dp", None), P("dp", "mp"))
    return jax.shard_map(
        local,
        mesh=mesh,
        in_specs=placed,
        out_specs=(P("dp", "mp"), P("dp", "mp"), P("dp", "mp"), P("dp", "mp")),
        check_vma=False,
    )
```

```python
import functools

import jax
import jax.numpy as jnp
from jax import lax
from jax.experimental import pallas as pl
from jax.experimental.pallas import tpu as pltpu
from jax.sharding import PartitionSpec as P

HEADS = 64
HS = 128
GROUP = 64
FEAT = HEADS * HS
EPSILON = 1e-06
SCALING = 1.0 / HS**0.5
LANES = 128
CHUNK = 16
VMEM_LIMIT = 8 * 1024 * 1024
WORK = 8 * 1024 * 1024
SLOTS = 5
OWN = (0, 2)
PARTNER = (1, 3, 4)


def routes(count):
    def side(i):
        return -4 if i & 2 == 0 else 4

    diagonal = (-3, -1, 1, 3)
    return {
        "y": [(i, i ^ 2) for i in range(count)],
        2: [(i, i ^ 1) for i in range(count)],
        3: [(i, (i + side(i)) % count) for i in range(count)],
        4: [(i, (i + diagonal[i & 3]) % count) for i in range(count)],
    }


def sent(array, route):
    return lax.ppermute(array, "dp", route)


def out_and_back(count):
    route = routes(count)
    back = {s: [(b, a) for a, b in route[s]] for s in (2, 3, 4)}

    return route, back, functools.partial(sent, route=route["y"])


def dot(a, b, left, right):
    return lax.dot_general(a, b, (((left,), (right,)), ((), ())), preferred_element_type=jnp.float32)


def group_numbers(place_ref, near_ref, count, groups):
    place = place_ref[0]
    one = 1 - 2 * (place & 1)
    two = 2 - 2 * (place & 2)
    numbers = []
    for offset in (0, two, one, -two, -one):
        block = lax.rem(place + offset + count, count)
        number = jnp.int32(-1)
        for g in range(groups):
            used = (near_ref[g, 0] == block) | (near_ref[g, 1] == block)
            number = jnp.where(used, g, number)
        numbers.append(number)
    return numbers


def rows_of(number):
    return pl.ds(pl.multiple_of(jnp.maximum(number, 0) * GROUP, GROUP), GROUP)


def to_row(x):
    return jnp.sum(x.T, axis=0, keepdims=True)


def to_columns(row):
    return jnp.broadcast_to(row, (row.shape[1], row.shape[1])).T


def tile(t):
    return slice(t * LANES, (t + 1) * LANES)


def squares_kernel(q_ref, squares_ref):
    x = q_ref[:, tile(0)].astype(jnp.float32)
    total = x * x
    for t in range(1, q_ref.shape[1] // LANES):
        x = q_ref[:, tile(t)].astype(jnp.float32)
        total = total + x * x
    squares_ref[...] = to_row(total)


def pick_kernel(slots, count, groups, place_ref, near_ref, g_ref, *slot_refs):
    numbers = group_numbers(place_ref, near_ref, count, groups)
    for s, slot_ref in zip(slots, slot_refs):
        slot_ref[...] = g_ref[rows_of(numbers[s])]


def added(refs):
    total = refs[0][...]
    for ref in refs[1:]:
        total = total + ref[...]
    return total


def inverse_columns(squares_refs):
    return to_columns(lax.rsqrt(added(squares_refs) / FEAT + EPSILON))


def prepare_queries_kernel(count, groups, place_ref, near_ref, q_ref, gain_ref, *refs):
    *squares_refs, normed_ref, _, _, _ = refs
    slot_refs = refs[-3:]
    numbers = group_numbers(place_ref, near_ref, count, groups)
    inverse = inverse_columns(squares_refs)
    for t in range(q_ref.shape[1] // LANES):
        x = q_ref[:, tile(t)].astype(jnp.float32)
        normed_ref[:, tile(t)] = (x * gain_ref[:, tile(t)] * inverse).astype(jnp.bfloat16)
    for slot_ref, number in zip(slot_refs, numbers[2:]):
        slot_ref[...] = normed_ref[rows_of(number)]


def slot_views(numbers, whole_ref, slot_refs):
    own = [whole_ref.at[rows_of(numbers[s])] for s in range(SLOTS - len(slot_refs))]
    return own + list(slot_refs)


def head(refs, slots, cols):
    return jnp.concatenate([refs[s][:, cols] for s in slots], axis=0)


def each_chunk(heads, unit, body):
    def step(i, carry):
        first = i * unit
        cols = [pl.ds(pl.multiple_of((first + h) * HS, HS), HS) for h in range(unit)]
        body(pl.ds(pl.multiple_of(first, unit), unit), cols)
        return carry

    lax.fori_loop(0, heads // unit, step, 0)


def scores_kernel(count, groups, place_ref, near_ref, *refs):
    numbers = group_numbers(place_ref, near_ref, count, groups)
    q_refs = slot_views(numbers, refs[0], refs[1:4])
    k_refs, stat_refs, weight_refs = refs[4:6], refs[6 : 6 + SLOTS], refs[6 + SLOTS :]

    def body(rows, cols):
        for slots, k_ref, weight_ref in zip((OWN, PARTNER), k_refs, weight_refs):
            scores = [dot(k_ref[:, c], head(q_refs, slots, c), 1, 1) * SCALING for c in cols]
            tops = [jnp.max(x, axis=0, keepdims=True) for x in scores]
            totals = []
            for c, x, top in zip(cols, scores, tops):
                weights = jnp.exp(x - top)
                weight_ref[c] = weights
                totals.append(jnp.sum(weights, axis=0, keepdims=True))
            tops = jnp.concatenate(tops, axis=0)
            totals = jnp.concatenate(totals, axis=0)
            for at, s in enumerate(slots):
                lanes = slice(at * GROUP, (at + 1) * GROUP)
                stat_refs[s][rows] = jnp.concatenate([tops[:, lanes], totals[:, lanes]], axis=1)

    each_chunk(stat_refs[0].shape[0], CHUNK, body)


def combine_scores_kernel(count, groups, place_ref, near_ref, *refs):
    stat_refs, back_refs = refs[:SLOTS], refs[SLOTS:]
    numbers = group_numbers(place_ref, near_ref, count, groups)
    heads = stat_refs[0].shape[0]
    shape = (heads, GROUP)
    tops = [r[:, 0:GROUP] for r in stat_refs]
    totals = [r[:, GROUP : 2 * GROUP] for r in stat_refs]
    number_of = [jnp.full(shape, n, jnp.int32) for n in numbers]
    lowest = jnp.full(shape, -jnp.inf, jnp.float32)
    zero = jnp.zeros(shape, jnp.float32)
    merged = []
    for g in range(groups):
        top, total = lowest, zero
        for s in range(SLOTS):
            top = jnp.maximum(top, jnp.where(number_of[s] == g, tops[s], lowest))
        for s in range(SLOTS):
            mine = number_of[s] == g
            factor = jnp.exp(jnp.where(mine, tops[s] - top, zero))
            total = total + jnp.where(mine, totals[s] * factor, zero)
        merged.append((top, 1.0 / total))
    for s in range(SLOTS):
        share = zero
        for g in range(groups):
            mine = number_of[s] == g
            factor = jnp.exp(jnp.where(mine, tops[s] - merged[g][0], zero))
            share = jnp.where(mine, factor * merged[g][1], share)
        back_refs[s][...] = jnp.concatenate([share, zero], axis=1)


def combine_centres_kernel(count, groups, place_ref, near_ref, *refs):
    stat_refs, back_refs = refs[:SLOTS], refs[SLOTS:]
    numbers = group_numbers(place_ref, near_ref, count, groups)
    shape = stat_refs[0].shape
    number_of = [jnp.full(shape, n, jnp.int32) for n in numbers]
    zero = jnp.zeros(shape, jnp.float32)
    totals = []
    for g in range(groups):
        total = zero
        for s in range(SLOTS):
            total = total + jnp.where(number_of[s] == g, stat_refs[s][...], zero)
        totals.append(total)
    for s in range(SLOTS):
        here = zero
        for g in range(groups):
            here = jnp.where(number_of[s] == g, totals[g], here)
        back_refs[s][...] = here


def stat_rows(stat_refs, slots, rows):
    return jnp.concatenate([stat_refs[s][rows, 0:GROUP] for s in slots], axis=1)


def probs_of(rows, slots, back_refs, weight_ref, cols):
    shares = stat_rows(back_refs, slots, rows)
    return [weight_ref[c] * shares[h : h + 1] for h, c in enumerate(cols)]


def centres_kernel(count, groups, place_ref, near_ref, *refs):
    numbers = group_numbers(place_ref, near_ref, count, groups)
    g_refs = slot_views(numbers, refs[0], refs[1:4])
    v_refs, weight_refs, back_refs = refs[4:6], refs[6:8], refs[8 : 8 + SLOTS]
    centre_refs = refs[8 + SLOTS : 8 + 2 * SLOTS]
    *product_refs, dv_ref = refs[8 + 2 * SLOTS :]

    def body(rows, cols):
        for slots, v_ref, weight_ref, product_ref in zip(
            (OWN, PARTNER), v_refs, weight_refs, product_refs
        ):
            products = [dot(v_ref[:, c], head(g_refs, slots, c), 1, 1) for c in cols]
            probs = probs_of(rows, slots, back_refs, weight_ref, cols)
            for c, x, p in zip(cols, products, probs):
                product_ref[c] = x
                if slots is PARTNER:
                    product = dot(p.astype(jnp.bfloat16), head(g_refs, slots, c), 1, 0)
                    dv_ref[:, c] = product.astype(jnp.bfloat16)
            centres = [jnp.sum(p * x, axis=0, keepdims=True) for p, x in zip(probs, products)]
            centres = jnp.concatenate(centres, axis=0)
            empty = jnp.zeros((centres.shape[0], GROUP), jnp.float32)
            for at, s in enumerate(slots):
                lanes = slice(at * GROUP, (at + 1) * GROUP)
                centre_refs[s][rows] = jnp.concatenate([centres[:, lanes], empty], axis=1)

    each_chunk(centre_refs[0].shape[0], CHUNK, body)


def context_kernel(*refs):
    v_refs, weight_refs, back_refs = refs[0:2], refs[2:4], refs[4 : 4 + SLOTS]
    ctx_refs = refs[4 + SLOTS :]

    def body(rows, cols):
        for slots, v_ref, weight_ref in zip((OWN, PARTNER), v_refs, weight_refs):
            probs = probs_of(rows, slots, back_refs, weight_ref, cols)
            for c, p in zip(cols, probs):
                context = dot(p.astype(jnp.bfloat16), v_ref[:, c], 0, 0).astype(jnp.bfloat16)
                for at, s in enumerate(slots):
                    ctx_refs[s][:, c] = context[at * GROUP : (at + 1) * GROUP]

    each_chunk(back_refs[0].shape[0], CHUNK, body)


def grad_scores_of(rows, slots, back_refs, centre_refs, weight_ref, product_ref, cols):
    probs = probs_of(rows, slots, back_refs, weight_ref, cols)
    centre = stat_rows(centre_refs, slots, rows)
    return probs, [
        (p * (product_ref[c] - centre[h : h + 1])).astype(jnp.bfloat16)
        for h, (c, p) in enumerate(zip(cols, probs))
    ]


def gradient_kernel(count, groups, place_ref, near_ref, *refs):
    numbers = group_numbers(place_ref, near_ref, count, groups)
    q_refs = slot_views(numbers, refs[0], refs[1:4])
    k_refs, weight_refs, product_refs, rest = refs[4:6], refs[6:8], refs[8:10], refs[10:]
    back_refs, centre_refs, grad_refs = (rest[i * SLOTS : (i + 1) * SLOTS] for i in range(3))
    dk_ref = rest[3 * SLOTS]

    def body(rows, cols):
        for slots, k_ref, weight_ref, product_ref in zip(
            (OWN, PARTNER), k_refs, weight_refs, product_refs
        ):
            _, lows = grad_scores_of(
                rows, slots, back_refs, centre_refs, weight_ref, product_ref, cols
            )
            for c, low in zip(cols, lows):
                grad = (dot(low, k_ref[:, c], 0, 0) * SCALING).astype(jnp.bfloat16)
                for at, s in enumerate(slots):
                    grad_refs[s][:, c] = grad[at * GROUP : (at + 1) * GROUP]
                if slots is PARTNER:
                    product = dot(low, head(q_refs, slots, c), 1, 0) * SCALING
                    dk_ref[:, c] = product.astype(jnp.bfloat16)

    each_chunk(back_refs[0].shape[0], CHUNK, body)


def own_kernel(count, groups, place_ref, near_ref, *refs):
    numbers = group_numbers(place_ref, near_ref, count, groups)
    normed_ref, q_ref, grad_ref, g_ref, weight_ref, product_ref = refs[:6]
    q_refs = dict(zip(OWN, (normed_ref.at[rows_of(numbers[0])], q_ref)))
    g_refs = dict(zip(OWN, (grad_ref.at[rows_of(numbers[0])], g_ref)))
    back_refs, centre_refs = dict(zip(OWN, refs[6:8])), dict(zip(OWN, refs[8:10]))
    far_dv_ref, far_dk_ref, dv_ref, dk_ref = refs[10:]

    def body(rows, cols):
        probs, lows = grad_scores_of(
            rows, OWN, back_refs, centre_refs, weight_ref, product_ref, cols
        )
        for c, p, low in zip(cols, probs, lows):
            total = dot(p.astype(jnp.bfloat16), head(g_refs, OWN, c), 1, 0)
            total = total + far_dv_ref[:, c].astype(jnp.float32)
            dv_ref[:, c] = total.astype(jnp.bfloat16)
            total = dot(low, head(q_refs, OWN, c), 1, 0) * SCALING
            total = total + far_dk_ref[:, c].astype(jnp.float32)
            dk_ref[:, c] = total.astype(jnp.bfloat16)

    each_chunk(refs[6].shape[0], CHUNK, body)


def gathered(weights, refs, t):
    total = None
    for s in range(SLOTS):
        part = weights[s] * refs[s][:, tile(t)].astype(jnp.float32)
        total = part if total is None else total + part
    return total


def weights_of(numbers, g):
    return [jnp.where(n == g, 1.0, 0.0) for n in numbers]


def attended_kernel(count, groups, place_ref, near_ref, *refs):
    ctx_refs, out_ref = refs[:SLOTS], refs[SLOTS]
    numbers = group_numbers(place_ref, near_ref, count, groups)
    for g in range(groups):
        weights = weights_of(numbers, g)
        rows = slice(g * GROUP, (g + 1) * GROUP)
        for t in range(out_ref.shape[1] // LANES):
            out_ref[rows, tile(t)] = gathered(weights, ctx_refs, t).astype(jnp.bfloat16)


def inner_kernel(count, groups, place_ref, near_ref, *refs):
    grad_refs = refs[:SLOTS]
    q_ref, gain_ref, scaled_ref, inner_ref = refs[SLOTS:]
    numbers = group_numbers(place_ref, near_ref, count, groups)
    totals = []
    for g in range(groups):
        weights = weights_of(numbers, g)
        rows = slice(g * GROUP, (g + 1) * GROUP)
        total = jnp.zeros((GROUP, LANES), jnp.float32)
        for t in range(q_ref.shape[1] // LANES):
            scaled = gathered(weights, grad_refs, t) * gain_ref[:, tile(t)]
            scaled_ref[rows, tile(t)] = scaled
            total = total + scaled * q_ref[rows, tile(t)].astype(jnp.float32)
        totals.append(total)
    inner_ref[...] = to_row(jnp.concatenate(totals, axis=0))


def finish_kernel(scaled_ref, q_ref, *refs):
    *sum_refs, dq_ref = refs
    half = len(sum_refs) // 2
    inverse = inverse_columns(sum_refs[:half])
    factor = inverse * inverse * inverse * to_columns(added(sum_refs[half:])) / FEAT
    for t in range(q_ref.shape[1] // LANES):
        x = q_ref[:, tile(t)].astype(jnp.float32)
        dq_ref[:, tile(t)] = (inverse * scaled_ref[:, tile(t)] - x * factor).astype(jnp.bfloat16)


def spread(array, axis):
    count = lax.axis_size(axis)
    shifts = [[(i, (i + k) % count) for i in range(count)] for k in range(1, count)]
    return [array] + [lax.ppermute(array, axis, shift) for shift in shifts]


def in_vmem(array):
    return pltpu.with_memory_space_constraint(array, pltpu.VMEM)


def after(values, *tokens):
    return lax.optimization_barrier((values, tokens))[0]


def kernel_call(body, name, outs, scratch=(), scalars=0, last=(), cost=0):
    vmem = pl.BlockSpec(memory_space=pltpu.VMEM)

    def call(*args):
        small, large = args[:scalars], [in_vmem(a) for a in args[scalars:]]
        shapes = [
            (jax.ShapeDtypeStruct if i in last else pltpu.VMEM)(shape, dtype)
            for i, (shape, dtype) in enumerate(outs)
        ]
        results = pl.pallas_call(
            body,
            in_specs=[pl.BlockSpec(memory_space=pltpu.SMEM)] * scalars + [vmem] * len(large),
            out_specs=[vmem] * len(outs),
            out_shape=shapes,
            scratch_shapes=list(scratch),
            name=name,
            cost_estimate=pl.CostEstimate(flops=0, bytes_accessed=cost, transcendentals=0),
            compiler_params=pltpu.CompilerParams(vmem_limit_bytes=VMEM_LIMIT),
        )(*small, *large)
        return list(results)

    return call


def local(queries, query_gain, keys, values, neighbours, d_out):
    rows, width = queries.shape
    heads = width // HS
    groups = rows // GROUP
    count = lax.axis_size("dp")
    route, back_route, across = out_and_back(count)
    place = jnp.full((1,), lax.axis_index("dp"), jnp.int32)
    gain = query_gain[None, :]

    slot = ((GROUP, width), jnp.bfloat16)
    tall = ((rows, width), jnp.bfloat16)
    row = ((1, rows), jnp.float32)
    stat = ((heads, LANES), jnp.float32)

    def out(part, s):
        return sent(part, route[s])

    def home(part, s):
        return sent(part, back_route[s])

    def go(parts):
        return [out(p, s) if s >= 2 else p for s, p in enumerate(parts)]

    def come(parts):
        return [home(p, s) if s >= 2 else p for s, p in enumerate(parts)]

    def placed(kernel, name, outs, scratch=(), last=(), cost=0):
        call = kernel_call(
            functools.partial(kernel, count, groups), name, outs, scratch, 2, last, cost
        )
        return functools.partial(call, place, neighbours)

    def picked(slots, array):
        return placed(functools.partial(pick_kernel, slots), "pick", [slot] * len(slots))(array)

    far_keys = across(keys)
    (squares,) = kernel_call(squares_kernel, "squares", [row])(queries)
    squares = spread(squares, "mp")
    normed, *q_parts = placed(
        prepare_queries_kernel, "prepare_queries", [tall] + [slot] * 3
    )(queries, gain, *squares)
    q_slots = [out(q, s) for q, s in zip(q_parts, (2, 3, 4))]
    far_values = across(values)
    g2, g3 = picked((2, 3), after(d_out, q_parts[2]))
    g2, g3 = out(g2, 2), out(g3, 3)

    own_scores = ((width, len(OWN) * GROUP), jnp.float32)
    far_scores = ((width, len(PARTNER) * GROUP), jnp.float32)
    *stats, own_weights, far_weights = placed(
        scores_kernel, "scores", [stat] * SLOTS + [own_scores, far_scores]
    )(normed, *q_slots, keys, far_keys)
    stats[2:] = after(stats[2:], g2, g3)
    stats = come(stats)
    (g4,) = picked((4,), after(d_out, *stats[2:]))
    g_slots = [g2, g3, out(g4, 4)]
    back = placed(combine_scores_kernel, "combine_scores", [stat] * SLOTS)(*stats)
    back = go(back)

    inputs = [d_out, *g_slots, values, far_values, own_weights, far_weights]
    contexts = kernel_call(context_kernel, "context", [slot] * SLOTS)(
        *inputs[-4:], after(back[0], g_slots[2]), *back[1:]
    )
    held = [after(back[0], contexts[0]), *back[1:]]
    *centres, own_products, far_products, far_dv = placed(
        centres_kernel, "centres", [stat] * SLOTS + [own_scores, far_scores, tall]
    )(*inputs, *held)
    contexts[2:4] = [home(contexts[s], s) for s in (2, 3)]
    far_dv = across(after(far_dv, contexts[2], contexts[3]))
    centres[2:] = after(centres[2:], contexts[2], contexts[3])
    centres = come(centres)
    centres = placed(combine_centres_kernel, "combine_centres", [stat] * SLOTS)(*centres)
    contexts[4] = home(after(contexts[4], centres[1]), 4)
    centres = go(centres)

    *grads, far_dk = placed(gradient_kernel, "gradient", [slot] * SLOTS + [tall])(
        normed, *q_slots, keys, far_keys, own_weights, far_weights, own_products, far_products,
        *back, *centres,
    )
    far_dk = across(after(far_dk, far_dv))
    grads[4] = after(grads[4], contexts[4])
    grads = come(grads)

    d_values, d_keys = placed(own_kernel, "own", [tall, tall], last=(0, 1))(
        normed, q_slots[0], d_out, g2, own_weights, own_products, back[0], back[2], centres[0], centres[2],
        far_dv, far_dk,
    )
    (attended,) = placed(attended_kernel, "attended", [tall], last=(0,))(*contexts)
    grads[2:] = after(grads[2:], attended, d_values)
    scaled, inner = placed(inner_kernel, "inner", [((rows, width), jnp.float32), row])(
        *grads, queries, gain
    )
    inner = spread(inner, "mp")
    (d_queries,) = kernel_call(finish_kernel, "finish", [tall], last=(0,))(
        scaled, queries, *squares, *inner
    )
    return (attended, d_queries, d_keys, d_values)


def solution(mesh):
    placed = (P("dp", "mp"), P("mp"), P("dp", "mp"), P("dp", "mp"), P("dp", None), P("dp", "mp"))
    return jax.shard_map(
        local,
        mesh=mesh,
        in_specs=placed,
        out_specs=(P("dp", "mp"), P("dp", "mp"), P("dp", "mp"), P("dp", "mp")),
        check_vma=False,
    )
```

```python
import functools

import jax
import jax.numpy as jnp
from jax import lax
from jax.experimental import pallas as pl
from jax.experimental.pallas import tpu as pltpu
from jax.sharding import PartitionSpec as P

HEADS = 64
HS = 128
GROUP = 64
FEAT = HEADS * HS
EPSILON = 1e-06
SCALING = 1.0 / HS**0.5
LANES = 128
CHUNK = 16
VMEM_LIMIT = 8 * 1024 * 1024
WORK = 8 * 1024 * 1024
SLOTS = 5
OWN = (0, 2)
PARTNER = (1, 3, 4)


def routes(count):
    def side(i):
        return -4 if i & 2 == 0 else 4

    diagonal = (-3, -1, 1, 3)
    return {
        "y": [(i, i ^ 2) for i in range(count)],
        2: [(i, i ^ 1) for i in range(count)],
        3: [(i, (i + side(i)) % count) for i in range(count)],
        4: [(i, (i + diagonal[i & 3]) % count) for i in range(count)],
    }


def sent(array, route):
    return lax.ppermute(array, "dp", route)


def out_and_back(count):
    route = routes(count)
    back = {s: [(b, a) for a, b in route[s]] for s in (2, 3, 4)}

    return route, back, functools.partial(sent, route=route["y"])


def dot(a, b, left, right):
    return lax.dot_general(a, b, (((left,), (right,)), ((), ())), preferred_element_type=jnp.float32)


def group_numbers(place_ref, near_ref, count, groups):
    place = place_ref[0]
    one = 1 - 2 * (place & 1)
    two = 2 - 2 * (place & 2)
    numbers = []
    for offset in (0, two, one, -two, -one):
        block = lax.rem(place + offset + count, count)
        number = jnp.int32(-1)
        for g in range(groups):
            used = (near_ref[g, 0] == block) | (near_ref[g, 1] == block)
            number = jnp.where(used, g, number)
        numbers.append(number)
    return numbers


def rows_of(number):
    return pl.ds(pl.multiple_of(jnp.maximum(number, 0) * GROUP, GROUP), GROUP)


def to_row(x):
    return jnp.sum(x.T, axis=0, keepdims=True)


def to_columns(row):
    return jnp.broadcast_to(row, (row.shape[1], row.shape[1])).T


def tile(t):
    return slice(t * LANES, (t + 1) * LANES)


def squares_kernel(q_ref, squares_ref):
    x = q_ref[:, tile(0)].astype(jnp.float32)
    total = x * x
    for t in range(1, q_ref.shape[1] // LANES):
        x = q_ref[:, tile(t)].astype(jnp.float32)
        total = total + x * x
    squares_ref[...] = to_row(total)


def pick_kernel(slots, count, groups, place_ref, near_ref, g_ref, *slot_refs):
    numbers = group_numbers(place_ref, near_ref, count, groups)
    for s, slot_ref in zip(slots, slot_refs):
        slot_ref[...] = g_ref[rows_of(numbers[s])]


def added(refs):
    total = refs[0][...]
    for ref in refs[1:]:
        total = total + ref[...]
    return total


def inverse_columns(squares_refs):
    return to_columns(lax.rsqrt(added(squares_refs) / FEAT + EPSILON))


def prepare_queries_kernel(count, groups, place_ref, near_ref, q_ref, gain_ref, *refs):
    *squares_refs, normed_ref, _, _, _ = refs
    slot_refs = refs[-3:]
    numbers = group_numbers(place_ref, near_ref, count, groups)
    inverse = inverse_columns(squares_refs)
    for t in range(q_ref.shape[1] // LANES):
        x = q_ref[:, tile(t)].astype(jnp.float32)
        normed_ref[:, tile(t)] = (x * gain_ref[:, tile(t)] * inverse).astype(jnp.bfloat16)
    for slot_ref, number in zip(slot_refs, numbers[2:]):
        slot_ref[...] = normed_ref[rows_of(number)]


def slot_views(numbers, whole_ref, slot_refs):
    own = [whole_ref.at[rows_of(numbers[s])] for s in range(SLOTS - len(slot_refs))]
    return own + list(slot_refs)


def head(refs, slots, cols):
    return jnp.concatenate([refs[s][:, cols] for s in slots], axis=0)


def each_chunk(heads, unit, body):
    def step(i, carry):
        first = i * unit
        cols = [pl.ds(pl.multiple_of((first + h) * HS, HS), HS) for h in range(unit)]
        body(pl.ds(pl.multiple_of(first, unit), unit), cols)
        return carry

    lax.fori_loop(0, heads // unit, step, 0)


def scores_kernel(count, groups, place_ref, near_ref, *refs):
    numbers = group_numbers(place_ref, near_ref, count, groups)
    q_refs = slot_views(numbers, refs[0], refs[1:4])
    k_refs, stat_refs, weight_refs = refs[4:6], refs[6 : 6 + SLOTS], refs[6 + SLOTS :]

    def body(rows, cols):
        for slots, k_ref, weight_ref in zip((OWN, PARTNER), k_refs, weight_refs):
            scores = [dot(k_ref[:, c], head(q_refs, slots, c), 1, 1) * SCALING for c in cols]
            tops = [jnp.max(x, axis=0, keepdims=True) for x in scores]
            totals = []
            for c, x, top in zip(cols, scores, tops):
                weights = jnp.exp(x - top)
                weight_ref[c] = weights
                totals.append(jnp.sum(weights, axis=0, keepdims=True))
            tops = jnp.concatenate(tops, axis=0)
            totals = jnp.concatenate(totals, axis=0)
            for at, s in enumerate(slots):
                lanes = slice(at * GROUP, (at + 1) * GROUP)
                stat_refs[s][rows] = jnp.concatenate([tops[:, lanes], totals[:, lanes]], axis=1)

    each_chunk(stat_refs[0].shape[0], CHUNK, body)


def combine_scores_kernel(count, groups, place_ref, near_ref, *refs):
    stat_refs, back_refs = refs[:SLOTS], refs[SLOTS:]
    numbers = group_numbers(place_ref, near_ref, count, groups)
    heads = stat_refs[0].shape[0]
    shape = (heads, GROUP)
    tops = [r[:, 0:GROUP] for r in stat_refs]
    totals = [r[:, GROUP : 2 * GROUP] for r in stat_refs]
    number_of = [jnp.full(shape, n, jnp.int32) for n in numbers]
    lowest = jnp.full(shape, -jnp.inf, jnp.float32)
    zero = jnp.zeros(shape, jnp.float32)
    merged = []
    for g in range(groups):
        top, total = lowest, zero
        for s in range(SLOTS):
            top = jnp.maximum(top, jnp.where(number_of[s] == g, tops[s], lowest))
        for s in range(SLOTS):
            mine = number_of[s] == g
            factor = jnp.exp(jnp.where(mine, tops[s] - top, zero))
            total = total + jnp.where(mine, totals[s] * factor, zero)
        merged.append((top, 1.0 / total))
    for s in range(SLOTS):
        share = zero
        for g in range(groups):
            mine = number_of[s] == g
            factor = jnp.exp(jnp.where(mine, tops[s] - merged[g][0], zero))
            share = jnp.where(mine, factor * merged[g][1], share)
        back_refs[s][...] = jnp.concatenate([share, zero], axis=1)


def combine_centres_kernel(count, groups, place_ref, near_ref, *refs):
    stat_refs, back_refs = refs[:SLOTS], refs[SLOTS:]
    numbers = group_numbers(place_ref, near_ref, count, groups)
    shape = stat_refs[0].shape
    number_of = [jnp.full(shape, n, jnp.int32) for n in numbers]
    zero = jnp.zeros(shape, jnp.float32)
    totals = []
    for g in range(groups):
        total = zero
        for s in range(SLOTS):
            total = total + jnp.where(number_of[s] == g, stat_refs[s][...], zero)
        totals.append(total)
    for s in range(SLOTS):
        here = zero
        for g in range(groups):
            here = jnp.where(number_of[s] == g, totals[g], here)
        back_refs[s][...] = here


def stat_rows(stat_refs, slots, rows):
    return jnp.concatenate([stat_refs[s][rows, 0:GROUP] for s in slots], axis=1)


def probs_of(rows, slots, back_refs, weight_ref, cols):
    shares = stat_rows(back_refs, slots, rows)
    return [weight_ref[c] * shares[h : h + 1] for h, c in enumerate(cols)]


def centres_kernel(count, groups, place_ref, near_ref, *refs):
    numbers = group_numbers(place_ref, near_ref, count, groups)
    g_refs = slot_views(numbers, refs[0], refs[1:4])
    v_refs, weight_refs, back_refs = refs[4:6], refs[6:8], refs[8 : 8 + SLOTS]
    centre_refs = refs[8 + SLOTS : 8 + 2 * SLOTS]
    *product_refs, dv_ref = refs[8 + 2 * SLOTS :]

    def body(rows, cols):
        for slots, v_ref, weight_ref, product_ref in zip(
            (OWN, PARTNER), v_refs, weight_refs, product_refs
        ):
            products = [dot(v_ref[:, c], head(g_refs, slots, c), 1, 1) for c in cols]
            probs = probs_of(rows, slots, back_refs, weight_ref, cols)
            for c, x, p in zip(cols, products, probs):
                product_ref[c] = x
                if slots is PARTNER:
                    product = dot(p.astype(jnp.bfloat16), head(g_refs, slots, c), 1, 0)
                    dv_ref[:, c] = product.astype(jnp.bfloat16)
            centres = [jnp.sum(p * x, axis=0, keepdims=True) for p, x in zip(probs, products)]
            centres = jnp.concatenate(centres, axis=0)
            empty = jnp.zeros((centres.shape[0], GROUP), jnp.float32)
            for at, s in enumerate(slots):
                lanes = slice(at * GROUP, (at + 1) * GROUP)
                centre_refs[s][rows] = jnp.concatenate([centres[:, lanes], empty], axis=1)

    each_chunk(centre_refs[0].shape[0], CHUNK, body)


def context_kernel(*refs):
    v_refs, weight_refs, back_refs = refs[0:2], refs[2:4], refs[4 : 4 + SLOTS]
    ctx_refs = refs[4 + SLOTS :]

    def body(rows, cols):
        for slots, v_ref, weight_ref in zip((OWN, PARTNER), v_refs, weight_refs):
            probs = probs_of(rows, slots, back_refs, weight_ref, cols)
            for c, p in zip(cols, probs):
                context = dot(p.astype(jnp.bfloat16), v_ref[:, c], 0, 0).astype(jnp.bfloat16)
                for at, s in enumerate(slots):
                    ctx_refs[s][:, c] = context[at * GROUP : (at + 1) * GROUP]

    each_chunk(back_refs[0].shape[0], CHUNK, body)


def grad_scores_of(rows, slots, back_refs, centre_refs, weight_ref, product_ref, cols):
    probs = probs_of(rows, slots, back_refs, weight_ref, cols)
    centre = stat_rows(centre_refs, slots, rows)
    return probs, [
        (p * (product_ref[c] - centre[h : h + 1])).astype(jnp.bfloat16)
        for h, (c, p) in enumerate(zip(cols, probs))
    ]


def gradient_kernel(count, groups, place_ref, near_ref, *refs):
    numbers = group_numbers(place_ref, near_ref, count, groups)
    q_refs = slot_views(numbers, refs[0], refs[1:4])
    k_refs, weight_refs, product_refs, rest = refs[4:6], refs[6:8], refs[8:10], refs[10:]
    back_refs, centre_refs, grad_refs = (rest[i * SLOTS : (i + 1) * SLOTS] for i in range(3))
    dk_ref = rest[3 * SLOTS]

    def body(rows, cols):
        for slots, k_ref, weight_ref, product_ref in zip(
            (OWN, PARTNER), k_refs, weight_refs, product_refs
        ):
            _, lows = grad_scores_of(
                rows, slots, back_refs, centre_refs, weight_ref, product_ref, cols
            )
            for c, low in zip(cols, lows):
                grad = (dot(low, k_ref[:, c], 0, 0) * SCALING).astype(jnp.bfloat16)
                for at, s in enumerate(slots):
                    grad_refs[s][:, c] = grad[at * GROUP : (at + 1) * GROUP]
                if slots is PARTNER:
                    product = dot(low, head(q_refs, slots, c), 1, 0) * SCALING
                    dk_ref[:, c] = product.astype(jnp.bfloat16)

    each_chunk(back_refs[0].shape[0], CHUNK, body)


def own_kernel(count, groups, place_ref, near_ref, *refs):
    numbers = group_numbers(place_ref, near_ref, count, groups)
    normed_ref, q_ref, grad_ref, g_ref, weight_ref, product_ref = refs[:6]
    q_refs = dict(zip(OWN, (normed_ref.at[rows_of(numbers[0])], q_ref)))
    g_refs = dict(zip(OWN, (grad_ref.at[rows_of(numbers[0])], g_ref)))
    back_refs, centre_refs = dict(zip(OWN, refs[6:8])), dict(zip(OWN, refs[8:10]))
    far_dv_ref, dv_ref, dk_ref = refs[10:]

    def body(rows, cols):
        probs, lows = grad_scores_of(
            rows, OWN, back_refs, centre_refs, weight_ref, product_ref, cols
        )
        for c, p, low in zip(cols, probs, lows):
            total = dot(p.astype(jnp.bfloat16), head(g_refs, OWN, c), 1, 0)
            total = total + far_dv_ref[:, c].astype(jnp.float32)
            dv_ref[:, c] = total.astype(jnp.bfloat16)
            dk_ref[:, c] = dot(low, head(q_refs, OWN, c), 1, 0) * SCALING

    each_chunk(refs[6].shape[0], CHUNK, body)


def add_kernel(own_ref, far_ref, out_ref):
    for t in range(out_ref.shape[1] // LANES):
        total = own_ref[:, tile(t)] + far_ref[:, tile(t)].astype(jnp.float32)
        out_ref[:, tile(t)] = total.astype(jnp.bfloat16)


def gathered(weights, refs, t):
    total = None
    for s in range(SLOTS):
        part = weights[s] * refs[s][:, tile(t)].astype(jnp.float32)
        total = part if total is None else total + part
    return total


def weights_of(numbers, g):
    return [jnp.where(n == g, 1.0, 0.0) for n in numbers]


def attended_kernel(count, groups, place_ref, near_ref, *refs):
    ctx_refs, out_ref = refs[:SLOTS], refs[SLOTS]
    numbers = group_numbers(place_ref, near_ref, count, groups)
    for g in range(groups):
        weights = weights_of(numbers, g)
        rows = slice(g * GROUP, (g + 1) * GROUP)
        for t in range(out_ref.shape[1] // LANES):
            out_ref[rows, tile(t)] = gathered(weights, ctx_refs, t).astype(jnp.bfloat16)


def inner_kernel(count, groups, place_ref, near_ref, *refs):
    grad_refs = refs[:SLOTS]
    q_ref, gain_ref, scaled_ref, inner_ref = refs[SLOTS:]
    numbers = group_numbers(place_ref, near_ref, count, groups)
    totals = []
    for g in range(groups):
        weights = weights_of(numbers, g)
        rows = slice(g * GROUP, (g + 1) * GROUP)
        total = jnp.zeros((GROUP, LANES), jnp.float32)
        for t in range(q_ref.shape[1] // LANES):
            scaled = gathered(weights, grad_refs, t) * gain_ref[:, tile(t)]
            scaled_ref[rows, tile(t)] = scaled
            total = total + scaled * q_ref[rows, tile(t)].astype(jnp.float32)
        totals.append(total)
    inner_ref[...] = to_row(jnp.concatenate(totals, axis=0))


def finish_kernel(scaled_ref, q_ref, *refs):
    *sum_refs, dq_ref = refs
    half = len(sum_refs) // 2
    inverse = inverse_columns(sum_refs[:half])
    factor = inverse * inverse * inverse * to_columns(added(sum_refs[half:])) / FEAT
    for t in range(q_ref.shape[1] // LANES):
        x = q_ref[:, tile(t)].astype(jnp.float32)
        dq_ref[:, tile(t)] = (inverse * scaled_ref[:, tile(t)] - x * factor).astype(jnp.bfloat16)


def spread(array, axis):
    count = lax.axis_size(axis)
    shifts = [[(i, (i + k) % count) for i in range(count)] for k in range(1, count)]
    return [array] + [lax.ppermute(array, axis, shift) for shift in shifts]


def in_vmem(array):
    return pltpu.with_memory_space_constraint(array, pltpu.VMEM)


def after(values, *tokens):
    return lax.optimization_barrier((values, tokens))[0]


def kernel_call(body, name, outs, scratch=(), scalars=0, last=(), cost=0):
    vmem = pl.BlockSpec(memory_space=pltpu.VMEM)

    def call(*args):
        small, large = args[:scalars], [in_vmem(a) for a in args[scalars:]]
        shapes = [
            (jax.ShapeDtypeStruct if i in last else pltpu.VMEM)(shape, dtype)
            for i, (shape, dtype) in enumerate(outs)
        ]
        results = pl.pallas_call(
            body,
            in_specs=[pl.BlockSpec(memory_space=pltpu.SMEM)] * scalars + [vmem] * len(large),
            out_specs=[vmem] * len(outs),
            out_shape=shapes,
            scratch_shapes=list(scratch),
            name=name,
            cost_estimate=pl.CostEstimate(flops=0, bytes_accessed=cost, transcendentals=0),
            compiler_params=pltpu.CompilerParams(vmem_limit_bytes=VMEM_LIMIT),
        )(*small, *large)
        return list(results)

    return call


def local(queries, query_gain, keys, values, neighbours, d_out):
    rows, width = queries.shape
    heads = width // HS
    groups = rows // GROUP
    count = lax.axis_size("dp")
    route, back_route, across = out_and_back(count)
    place = jnp.full((1,), lax.axis_index("dp"), jnp.int32)
    gain = query_gain[None, :]

    slot = ((GROUP, width), jnp.bfloat16)
    tall = ((rows, width), jnp.bfloat16)
    row = ((1, rows), jnp.float32)
    stat = ((heads, LANES), jnp.float32)

    def out(part, s):
        return sent(part, route[s])

    def home(part, s):
        return sent(part, back_route[s])

    def go(parts):
        return [out(p, s) if s >= 2 else p for s, p in enumerate(parts)]

    def come(parts):
        return [home(p, s) if s >= 2 else p for s, p in enumerate(parts)]

    def placed(kernel, name, outs, scratch=(), last=(), cost=0):
        call = kernel_call(
            functools.partial(kernel, count, groups), name, outs, scratch, 2, last, cost
        )
        return functools.partial(call, place, neighbours)

    def picked(slots, array):
        return placed(functools.partial(pick_kernel, slots), "pick", [slot] * len(slots))(array)

    far_keys = across(keys)
    (squares,) = kernel_call(squares_kernel, "squares", [row])(queries)
    squares = spread(squares, "mp")
    normed, *q_parts = placed(
        prepare_queries_kernel, "prepare_queries", [tall] + [slot] * 3
    )(queries, gain, *squares)
    q_slots = [out(q, s) for q, s in zip(q_parts, (2, 3, 4))]
    far_values = across(values)
    g2, g3 = picked((2, 3), after(d_out, q_parts[2]))
    g2, g3 = out(g2, 2), out(g3, 3)

    own_scores = ((width, len(OWN) * GROUP), jnp.float32)
    far_scores = ((width, len(PARTNER) * GROUP), jnp.float32)
    *stats, own_weights, far_weights = placed(
        scores_kernel, "scores", [stat] * SLOTS + [own_scores, far_scores]
    )(normed, *q_slots, keys, far_keys)
    stats[2:] = after(stats[2:], g2, g3)
    stats = come(stats)
    (g4,) = picked((4,), after(d_out, *stats[2:]))
    g_slots = [g2, g3, out(g4, 4)]
    back = placed(combine_scores_kernel, "combine_scores", [stat] * SLOTS)(*stats)
    back = go(back)

    inputs = [d_out, *g_slots, values, far_values, own_weights, far_weights]
    contexts = kernel_call(context_kernel, "context", [slot] * SLOTS)(
        *inputs[-4:], after(back[0], g_slots[2]), *back[1:]
    )
    held = [after(back[0], contexts[0]), *back[1:]]
    *centres, own_products, far_products, far_dv = placed(
        centres_kernel, "centres", [stat] * SLOTS + [own_scores, far_scores, tall]
    )(*inputs, *held)
    contexts[2:4] = [home(contexts[s], s) for s in (2, 3)]
    far_dv = across(after(far_dv, contexts[2], contexts[3]))
    centres[2:] = after(centres[2:], contexts[2], contexts[3])
    centres = come(centres)
    centres = placed(combine_centres_kernel, "combine_centres", [stat] * SLOTS)(*centres)
    contexts[4] = home(after(contexts[4], centres[1]), 4)
    centres = go(centres)

    *grads, far_dk = placed(gradient_kernel, "gradient", [slot] * SLOTS + [tall])(
        normed, *q_slots, keys, far_keys, own_weights, far_weights, own_products, far_products,
        *back, *centres,
    )
    far_dk = across(after(far_dk, far_dv))
    grads[2:] = after(grads[2:], contexts[4])
    grads = come(grads)

    d_values, own_dk = placed(
        own_kernel, "own", [tall, ((rows, width), jnp.float32)], last=(0,)
    )(
        normed, q_slots[0], d_out, g2, own_weights, own_products, back[0], back[2], centres[0],
        centres[2], far_dv,
    )
    far_dk = after(far_dk, d_values)
    (d_keys,) = kernel_call(add_kernel, "add", [tall], last=(0,))(own_dk, far_dk)
    (attended,) = placed(attended_kernel, "attended", [tall], last=(0,))(*contexts)
    grads[2:] = after(grads[2:], attended, d_values, d_keys)
    scaled, inner = placed(inner_kernel, "inner", [((rows, width), jnp.float32), row])(
        *grads, queries, gain
    )
    inner = spread(inner, "mp")
    (d_queries,) = kernel_call(finish_kernel, "finish", [tall], last=(0,))(
        scaled, queries, *squares, *inner
    )
    return (attended, d_queries, d_keys, d_values)


def solution(mesh):
    placed = (P("dp", "mp"), P("mp"), P("dp", "mp"), P("dp", "mp"), P("dp", None), P("dp", "mp"))
    return jax.shard_map(
        local,
        mesh=mesh,
        in_specs=placed,
        out_specs=(P("dp", "mp"), P("dp", "mp"), P("dp", "mp"), P("dp", "mp")),
        check_vma=False,
    )
```

```python
import functools

import jax
import jax.numpy as jnp
from jax import lax
from jax.experimental import pallas as pl
from jax.experimental.pallas import tpu as pltpu
from jax.sharding import PartitionSpec as P

HEADS = 64
HS = 128
GROUP = 64
FEAT = HEADS * HS
EPSILON = 1e-06
SCALING = 1.0 / HS**0.5
LANES = 128
CHUNK = 16
VMEM_LIMIT = 8 * 1024 * 1024
WORK = 8 * 1024 * 1024
SLOTS = 5
OWN = (0, 2)
PARTNER = (1, 3, 4)


def routes(count):
    def side(i):
        return -4 if i & 2 == 0 else 4

    diagonal = (-3, -1, 1, 3)
    return {
        "y": [(i, i ^ 2) for i in range(count)],
        2: [(i, i ^ 1) for i in range(count)],
        3: [(i, (i + side(i)) % count) for i in range(count)],
        4: [(i, (i + diagonal[i & 3]) % count) for i in range(count)],
    }


def sent(array, route):
    return lax.ppermute(array, "dp", route)


def out_and_back(count):
    route = routes(count)
    back = {s: [(b, a) for a, b in route[s]] for s in (2, 3, 4)}

    return route, back, functools.partial(sent, route=route["y"])


def dot(a, b, left, right):
    return lax.dot_general(a, b, (((left,), (right,)), ((), ())), preferred_element_type=jnp.float32)


def group_numbers(place_ref, near_ref, count, groups):
    place = place_ref[0]
    one = 1 - 2 * (place & 1)
    two = 2 - 2 * (place & 2)
    numbers = []
    for offset in (0, two, one, -two, -one):
        block = lax.rem(place + offset + count, count)
        number = jnp.int32(-1)
        for g in range(groups):
            used = (near_ref[g, 0] == block) | (near_ref[g, 1] == block)
            number = jnp.where(used, g, number)
        numbers.append(number)
    return numbers


def rows_of(number):
    return pl.ds(pl.multiple_of(jnp.maximum(number, 0) * GROUP, GROUP), GROUP)


def to_row(x):
    return jnp.sum(x.T, axis=0, keepdims=True)


def to_columns(row):
    return jnp.broadcast_to(row, (row.shape[1], row.shape[1])).T


def tile(t):
    return slice(t * LANES, (t + 1) * LANES)


def squares_kernel(q_ref, squares_ref):
    x = q_ref[:, tile(0)].astype(jnp.float32)
    total = x * x
    for t in range(1, q_ref.shape[1] // LANES):
        x = q_ref[:, tile(t)].astype(jnp.float32)
        total = total + x * x
    squares_ref[...] = to_row(total)


def pick_kernel(slots, count, groups, place_ref, near_ref, g_ref, *slot_refs):
    numbers = group_numbers(place_ref, near_ref, count, groups)
    for s, slot_ref in zip(slots, slot_refs):
        slot_ref[...] = g_ref[rows_of(numbers[s])]


def added(refs):
    total = refs[0][...]
    for ref in refs[1:]:
        total = total + ref[...]
    return total


def inverse_columns(squares_refs):
    return to_columns(lax.rsqrt(added(squares_refs) / FEAT + EPSILON))


def prepare_queries_kernel(count, groups, place_ref, near_ref, q_ref, gain_ref, *refs):
    *squares_refs, normed_ref, _, _, _ = refs
    slot_refs = refs[-3:]
    numbers = group_numbers(place_ref, near_ref, count, groups)
    inverse = inverse_columns(squares_refs)
    for t in range(q_ref.shape[1] // LANES):
        x = q_ref[:, tile(t)].astype(jnp.float32)
        normed_ref[:, tile(t)] = (x * gain_ref[:, tile(t)] * inverse).astype(jnp.bfloat16)
    for slot_ref, number in zip(slot_refs, numbers[2:]):
        slot_ref[...] = normed_ref[rows_of(number)]


def slot_views(numbers, whole_ref, slot_refs):
    own = [whole_ref.at[rows_of(numbers[s])] for s in range(SLOTS - len(slot_refs))]
    return own + list(slot_refs)


def head(refs, slots, cols):
    return jnp.concatenate([refs[s][:, cols] for s in slots], axis=0)


def each_chunk(heads, unit, body):
    def step(i, carry):
        first = i * unit
        cols = [pl.ds(pl.multiple_of((first + h) * HS, HS), HS) for h in range(unit)]
        body(pl.ds(pl.multiple_of(first, unit), unit), cols)
        return carry

    lax.fori_loop(0, heads // unit, step, 0)


def scores_kernel(count, groups, place_ref, near_ref, *refs):
    numbers = group_numbers(place_ref, near_ref, count, groups)
    q_refs = slot_views(numbers, refs[0], refs[1:4])
    k_refs, stat_refs, weight_refs = refs[4:6], refs[6 : 6 + SLOTS], refs[6 + SLOTS :]

    def body(rows, cols):
        for slots, k_ref, weight_ref in zip((OWN, PARTNER), k_refs, weight_refs):
            scores = [dot(k_ref[:, c], head(q_refs, slots, c), 1, 1) * SCALING for c in cols]
            tops = [jnp.max(x, axis=0, keepdims=True) for x in scores]
            totals = []
            for c, x, top in zip(cols, scores, tops):
                weights = jnp.exp(x - top)
                weight_ref[c] = weights
                totals.append(jnp.sum(weights, axis=0, keepdims=True))
            tops = jnp.concatenate(tops, axis=0)
            totals = jnp.concatenate(totals, axis=0)
            for at, s in enumerate(slots):
                lanes = slice(at * GROUP, (at + 1) * GROUP)
                stat_refs[s][rows] = jnp.concatenate([tops[:, lanes], totals[:, lanes]], axis=1)

    each_chunk(stat_refs[0].shape[0], CHUNK, body)


def combine_scores_kernel(count, groups, place_ref, near_ref, *refs):
    stat_refs, back_refs = refs[:SLOTS], refs[SLOTS:]
    numbers = group_numbers(place_ref, near_ref, count, groups)
    heads = stat_refs[0].shape[0]
    shape = (heads, GROUP)
    tops = [r[:, 0:GROUP] for r in stat_refs]
    totals = [r[:, GROUP : 2 * GROUP] for r in stat_refs]
    number_of = [jnp.full(shape, n, jnp.int32) for n in numbers]
    lowest = jnp.full(shape, -jnp.inf, jnp.float32)
    zero = jnp.zeros(shape, jnp.float32)
    merged = []
    for g in range(groups):
        top, total = lowest, zero
        for s in range(SLOTS):
            top = jnp.maximum(top, jnp.where(number_of[s] == g, tops[s], lowest))
        for s in range(SLOTS):
            mine = number_of[s] == g
            factor = jnp.exp(jnp.where(mine, tops[s] - top, zero))
            total = total + jnp.where(mine, totals[s] * factor, zero)
        merged.append((top, 1.0 / total))
    for s in range(SLOTS):
        share = zero
        for g in range(groups):
            mine = number_of[s] == g
            factor = jnp.exp(jnp.where(mine, tops[s] - merged[g][0], zero))
            share = jnp.where(mine, factor * merged[g][1], share)
        back_refs[s][...] = jnp.concatenate([share, zero], axis=1)


def combine_centres_kernel(count, groups, place_ref, near_ref, *refs):
    stat_refs, back_refs = refs[:SLOTS], refs[SLOTS:]
    numbers = group_numbers(place_ref, near_ref, count, groups)
    shape = stat_refs[0].shape
    number_of = [jnp.full(shape, n, jnp.int32) for n in numbers]
    zero = jnp.zeros(shape, jnp.float32)
    totals = []
    for g in range(groups):
        total = zero
        for s in range(SLOTS):
            total = total + jnp.where(number_of[s] == g, stat_refs[s][...], zero)
        totals.append(total)
    for s in range(SLOTS):
        here = zero
        for g in range(groups):
            here = jnp.where(number_of[s] == g, totals[g], here)
        back_refs[s][...] = here


def stat_rows(stat_refs, slots, rows):
    return jnp.concatenate([stat_refs[s][rows, 0:GROUP] for s in slots], axis=1)


def probs_of(rows, slots, back_refs, weight_ref, cols):
    shares = stat_rows(back_refs, slots, rows)
    return [weight_ref[c] * shares[h : h + 1] for h, c in enumerate(cols)]


def centres_kernel(count, groups, place_ref, near_ref, *refs):
    numbers = group_numbers(place_ref, near_ref, count, groups)
    g_refs = slot_views(numbers, refs[0], refs[1:4])
    v_refs, weight_refs, back_refs = refs[4:6], refs[6:8], refs[8 : 8 + SLOTS]
    centre_refs = refs[8 + SLOTS : 8 + 2 * SLOTS]
    *product_refs, dv_ref = refs[8 + 2 * SLOTS :]

    def body(rows, cols):
        for slots, v_ref, weight_ref, product_ref in zip(
            (OWN, PARTNER), v_refs, weight_refs, product_refs
        ):
            products = [dot(v_ref[:, c], head(g_refs, slots, c), 1, 1) for c in cols]
            probs = probs_of(rows, slots, back_refs, weight_ref, cols)
            for c, x, p in zip(cols, products, probs):
                product_ref[c] = x
                if slots is PARTNER:
                    product = dot(p.astype(jnp.bfloat16), head(g_refs, slots, c), 1, 0)
                    dv_ref[:, c] = product.astype(jnp.bfloat16)
            centres = [jnp.sum(p * x, axis=0, keepdims=True) for p, x in zip(probs, products)]
            centres = jnp.concatenate(centres, axis=0)
            empty = jnp.zeros((centres.shape[0], GROUP), jnp.float32)
            for at, s in enumerate(slots):
                lanes = slice(at * GROUP, (at + 1) * GROUP)
                centre_refs[s][rows] = jnp.concatenate([centres[:, lanes], empty], axis=1)

    each_chunk(centre_refs[0].shape[0], CHUNK, body)


def context_kernel(*refs):
    v_refs, weight_refs, back_refs = refs[0:2], refs[2:4], refs[4 : 4 + SLOTS]
    ctx_refs = refs[4 + SLOTS :]

    def body(rows, cols):
        for slots, v_ref, weight_ref in zip((OWN, PARTNER), v_refs, weight_refs):
            probs = probs_of(rows, slots, back_refs, weight_ref, cols)
            for c, p in zip(cols, probs):
                context = dot(p.astype(jnp.bfloat16), v_ref[:, c], 0, 0).astype(jnp.bfloat16)
                for at, s in enumerate(slots):
                    ctx_refs[s][:, c] = context[at * GROUP : (at + 1) * GROUP]

    each_chunk(back_refs[0].shape[0], CHUNK, body)


def grad_scores_of(rows, slots, back_refs, centre_refs, weight_ref, product_ref, cols):
    probs = probs_of(rows, slots, back_refs, weight_ref, cols)
    centre = stat_rows(centre_refs, slots, rows)
    return probs, [
        (p * (product_ref[c] - centre[h : h + 1])).astype(jnp.bfloat16)
        for h, (c, p) in enumerate(zip(cols, probs))
    ]


def gradient_kernel(count, groups, place_ref, near_ref, *refs):
    numbers = group_numbers(place_ref, near_ref, count, groups)
    q_refs = slot_views(numbers, refs[0], refs[1:4])
    k_refs, weight_refs, product_refs, rest = refs[4:6], refs[6:8], refs[8:10], refs[10:]
    back_refs, centre_refs, grad_refs = (rest[i * SLOTS : (i + 1) * SLOTS] for i in range(3))
    dk_ref = rest[3 * SLOTS]

    def body(rows, cols):
        for slots, k_ref, weight_ref, product_ref in zip(
            (OWN, PARTNER), k_refs, weight_refs, product_refs
        ):
            _, lows = grad_scores_of(
                rows, slots, back_refs, centre_refs, weight_ref, product_ref, cols
            )
            for c, low in zip(cols, lows):
                grad = (dot(low, k_ref[:, c], 0, 0) * SCALING).astype(jnp.bfloat16)
                for at, s in enumerate(slots):
                    grad_refs[s][:, c] = grad[at * GROUP : (at + 1) * GROUP]
                if slots is PARTNER:
                    product = dot(low, head(q_refs, slots, c), 1, 0) * SCALING
                    dk_ref[:, c] = product.astype(jnp.bfloat16)

    each_chunk(back_refs[0].shape[0], CHUNK, body)


def own_kernel(count, groups, place_ref, near_ref, *refs):
    numbers = group_numbers(place_ref, near_ref, count, groups)
    normed_ref, q_ref, grad_ref, g_ref, weight_ref, product_ref = refs[:6]
    q_refs = dict(zip(OWN, (normed_ref.at[rows_of(numbers[0])], q_ref)))
    g_refs = dict(zip(OWN, (grad_ref.at[rows_of(numbers[0])], g_ref)))
    back_refs, centre_refs = dict(zip(OWN, refs[6:8])), dict(zip(OWN, refs[8:10]))
    far_dv_ref, dv_ref, dk_ref = refs[10:]

    def body(rows, cols):
        probs, lows = grad_scores_of(
            rows, OWN, back_refs, centre_refs, weight_ref, product_ref, cols
        )
        for c, p, low in zip(cols, probs, lows):
            total = dot(p.astype(jnp.bfloat16), head(g_refs, OWN, c), 1, 0)
            total = total + far_dv_ref[:, c].astype(jnp.float32)
            dv_ref[:, c] = total.astype(jnp.bfloat16)
            dk_ref[:, c] = dot(low, head(q_refs, OWN, c), 1, 0) * SCALING

    each_chunk(refs[6].shape[0], CHUNK, body)


def add_kernel(own_ref, far_ref, out_ref):
    for t in range(out_ref.shape[1] // LANES):
        total = own_ref[:, tile(t)] + far_ref[:, tile(t)].astype(jnp.float32)
        out_ref[:, tile(t)] = total.astype(jnp.bfloat16)


def gathered(weights, refs, t):
    total = None
    for s in range(SLOTS):
        part = weights[s] * refs[s][:, tile(t)].astype(jnp.float32)
        total = part if total is None else total + part
    return total


def weights_of(numbers, g):
    return [jnp.where(n == g, 1.0, 0.0) for n in numbers]


def attended_kernel(count, groups, place_ref, near_ref, *refs):
    ctx_refs, out_ref = refs[:SLOTS], refs[SLOTS]
    numbers = group_numbers(place_ref, near_ref, count, groups)
    for g in range(groups):
        weights = weights_of(numbers, g)
        rows = slice(g * GROUP, (g + 1) * GROUP)
        for t in range(out_ref.shape[1] // LANES):
            out_ref[rows, tile(t)] = gathered(weights, ctx_refs, t).astype(jnp.bfloat16)


def inner_kernel(count, groups, place_ref, near_ref, *refs):
    grad_refs = refs[:SLOTS]
    q_ref, gain_ref, scaled_ref, inner_ref = refs[SLOTS:]
    numbers = group_numbers(place_ref, near_ref, count, groups)
    totals = []
    for g in range(groups):
        weights = weights_of(numbers, g)
        rows = slice(g * GROUP, (g + 1) * GROUP)
        total = jnp.zeros((GROUP, LANES), jnp.float32)
        for t in range(q_ref.shape[1] // LANES):
            scaled = gathered(weights, grad_refs, t) * gain_ref[:, tile(t)]
            scaled_ref[rows, tile(t)] = scaled
            total = total + scaled * q_ref[rows, tile(t)].astype(jnp.float32)
        totals.append(total)
    inner_ref[...] = to_row(jnp.concatenate(totals, axis=0))


def finish_kernel(scaled_ref, q_ref, *refs):
    *sum_refs, dq_ref = refs
    half = len(sum_refs) // 2
    inverse = inverse_columns(sum_refs[:half])
    factor = inverse * inverse * inverse * to_columns(added(sum_refs[half:])) / FEAT
    for t in range(q_ref.shape[1] // LANES):
        x = q_ref[:, tile(t)].astype(jnp.float32)
        dq_ref[:, tile(t)] = (inverse * scaled_ref[:, tile(t)] - x * factor).astype(jnp.bfloat16)


def spread(array, axis):
    count = lax.axis_size(axis)
    shifts = [[(i, (i + k) % count) for i in range(count)] for k in range(1, count)]
    return [array] + [lax.ppermute(array, axis, shift) for shift in shifts]


def in_vmem(array):
    return pltpu.with_memory_space_constraint(array, pltpu.VMEM)


def after(values, *tokens):
    return lax.optimization_barrier((values, tokens))[0]


def kernel_call(body, name, outs, scratch=(), scalars=0, last=(), cost=0):
    vmem = pl.BlockSpec(memory_space=pltpu.VMEM)

    def call(*args):
        small, large = args[:scalars], [in_vmem(a) for a in args[scalars:]]
        shapes = [
            (jax.ShapeDtypeStruct if i in last else pltpu.VMEM)(shape, dtype)
            for i, (shape, dtype) in enumerate(outs)
        ]
        results = pl.pallas_call(
            body,
            in_specs=[pl.BlockSpec(memory_space=pltpu.SMEM)] * scalars + [vmem] * len(large),
            out_specs=[vmem] * len(outs),
            out_shape=shapes,
            scratch_shapes=list(scratch),
            name=name,
            cost_estimate=pl.CostEstimate(flops=0, bytes_accessed=cost, transcendentals=0),
            compiler_params=pltpu.CompilerParams(vmem_limit_bytes=VMEM_LIMIT),
        )(*small, *large)
        return list(results)

    return call


def local(queries, query_gain, keys, values, neighbours, d_out):
    rows, width = queries.shape
    heads = width // HS
    groups = rows // GROUP
    count = lax.axis_size("dp")
    route, back_route, across = out_and_back(count)
    place = jnp.full((1,), lax.axis_index("dp"), jnp.int32)
    gain = query_gain[None, :]

    slot = ((GROUP, width), jnp.bfloat16)
    tall = ((rows, width), jnp.bfloat16)
    row = ((1, rows), jnp.float32)
    stat = ((heads, LANES), jnp.float32)

    def out(part, s):
        return sent(part, route[s])

    def home(part, s):
        return sent(part, back_route[s])

    def go(parts):
        return [out(p, s) if s >= 2 else p for s, p in enumerate(parts)]

    def come(parts):
        return [home(p, s) if s >= 2 else p for s, p in enumerate(parts)]

    def placed(kernel, name, outs, scratch=(), last=(), cost=0):
        call = kernel_call(
            functools.partial(kernel, count, groups), name, outs, scratch, 2, last, cost
        )
        return functools.partial(call, place, neighbours)

    def picked(slots, array):
        return placed(functools.partial(pick_kernel, slots), "pick", [slot] * len(slots))(array)

    far_keys = across(keys)
    (squares,) = kernel_call(squares_kernel, "squares", [row])(queries)
    squares = spread(squares, "mp")
    normed, *q_parts = placed(
        prepare_queries_kernel, "prepare_queries", [tall] + [slot] * 3
    )(queries, gain, *squares)
    q_slots = [out(q, s) for q, s in zip(q_parts, (2, 3, 4))]
    far_values = across(values)
    g2, g3 = picked((2, 3), after(d_out, q_parts[2]))
    g2, g3 = out(g2, 2), out(g3, 3)

    own_scores = ((width, len(OWN) * GROUP), jnp.float32)
    far_scores = ((width, len(PARTNER) * GROUP), jnp.float32)
    *stats, own_weights, far_weights = placed(
        scores_kernel, "scores", [stat] * SLOTS + [own_scores, far_scores]
    )(normed, *q_slots, keys, far_keys)
    stats[2:] = after(stats[2:], g2, g3)
    stats = come(stats)
    (g4,) = picked((4,), after(d_out, *stats[2:]))
    g_slots = [g2, g3, out(g4, 4)]
    back = placed(combine_scores_kernel, "combine_scores", [stat] * SLOTS)(*stats)
    back = go(back)

    inputs = [d_out, *g_slots, values, far_values, own_weights, far_weights]
    contexts = kernel_call(context_kernel, "context", [slot] * SLOTS)(
        *inputs[-4:], after(back[0], g_slots[2]), *back[1:]
    )
    held = [after(back[0], contexts[0]), *back[1:]]
    *centres, own_products, far_products, far_dv = placed(
        centres_kernel, "centres", [stat] * SLOTS + [own_scores, far_scores, tall]
    )(*inputs, *held)
    contexts[2:4] = [home(contexts[s], s) for s in (2, 3)]
    far_dv = across(after(far_dv, contexts[2], contexts[3]))
    centres[2:] = after(centres[2:], contexts[2], contexts[3])
    centres = come(centres)
    centres = placed(combine_centres_kernel, "combine_centres", [stat] * SLOTS)(*centres)
    contexts[4] = home(after(contexts[4], centres[1]), 4)
    centres = go(centres)

    *grads, far_dk = placed(gradient_kernel, "gradient", [slot] * SLOTS + [tall])(
        normed, *q_slots, keys, far_keys, own_weights, far_weights, own_products, far_products,
        *back, *centres,
    )
    far_dk = across(after(far_dk, contexts[4]))
    grads[2:] = after(grads[2:], contexts[4])
    grads = come(grads)

    d_values, own_dk = placed(
        own_kernel, "own", [tall, ((rows, width), jnp.float32)], last=(0,)
    )(
        normed, q_slots[0], d_out, g2, own_weights, own_products, back[0], back[2], centres[0],
        centres[2], far_dv,
    )
    far_dk = after(far_dk, d_values)
    (d_keys,) = kernel_call(add_kernel, "add", [tall], last=(0,))(own_dk, far_dk)
    (attended,) = placed(attended_kernel, "attended", [tall], last=(0,))(*contexts)
    grads[2:] = after(grads[2:], attended, d_values, d_keys)
    scaled, inner = placed(inner_kernel, "inner", [((rows, width), jnp.float32), row])(
        *grads, queries, gain
    )
    inner = spread(inner, "mp")
    (d_queries,) = kernel_call(finish_kernel, "finish", [tall], last=(0,))(
        scaled, queries, *squares, *inner
    )
    return (attended, d_queries, d_keys, d_values)


def solution(mesh):
    placed = (P("dp", "mp"), P("mp"), P("dp", "mp"), P("dp", "mp"), P("dp", None), P("dp", "mp"))
    return jax.shard_map(
        local,
        mesh=mesh,
        in_specs=placed,
        out_specs=(P("dp", "mp"), P("dp", "mp"), P("dp", "mp"), P("dp", "mp")),
        check_vma=False,
    )
```
